32 devices in a mesh: expert: 16 (over z, y, x), dp: 2 (over core).
Axes of the slice: x: 2, y: 2, z: 4, core: 2. Of those that a mesh axis runs over, the one named last changes fastest.
Arguments:
- tokens: bfloat16 [4096, 7168], P(('expert', 'dp')), may hold values from -6 to 6
- cotangent: bfloat16 [4096, 7168], P(('expert', 'dp')), may hold values from -6 to 6
- logits: float32 [4096, 32], P(('expert', 'dp')), may hold values from -8 to 8
- expert_ids: int32 [4096, 8], P(('expert', 'dp')), may hold values from 0 to 31, all different within a row; in each aligned block of 128 rows (0 to 127, 128 to 255, ...) at most 40 rows name the same one
- gate_proj: bfloat16 [16, 7168, 128], P('expert'), may hold values from -0.0625 to 0.0625
- up_proj: bfloat16 [16, 7168, 128], P('expert'), may hold values from -0.0625 to 0.0625
- down_proj: bfloat16 [16, 128, 7168], P('expert'), may hold values from -0.125 to 0.125
Outputs:
- token_grad: bfloat16 [4096, 7168], P(('expert', 'dp'))
- logit_grad: float32 [4096, 32], P(('expert', 'dp'))
- down_grad: bfloat16 [16, 128, 7168], P('expert', None, 'dp')
The draws below stay inside these ranges and needn't reach their ends.
Inputs may be any that keep to these rules, and one draw needn't show every extreme that they name: `expert_ids`: each row names 8 different experts. Within the 128 rows of one device no expert is named more than 40 times, a bound that some block reaches.
All inputs are finite; a program needn't handle non-finite values.
Results may differ from the reference program's by a relative error of at most 0.012.
Values may be sent and summed in bfloat16 or wider, within the bound.
No kernel may reach another device: no remote copies, remote signals or barrier semaphores. Data moves between devices by JAX's collectives and lax.ppermute only.
A program may use at most 192 MiB of HBM per device.

```python
import math
import jax
import jax.numpy as jnp
import numpy as np
from jax import lax

D = 7168
FF = 2048
TOP = 8
SPLIT = 16
TOK_DEV = 128
FF_DEV = 128
HELD = 1
EXPERTS = 32
CAP = 40
TOKENS = 4096


def steps_of(own_key, shape, cuts, smallest, top_value):
    factor_of, own = 1.0, jax.random.fold_in(own_key, 6)
    for axis_at, blocks in cuts:
        steps = jnp.exp(jax.random.uniform(jax.random.fold_in(own, axis_at), (blocks,), jnp.float32, smallest / len(cuts), top_value / len(cuts)))
        factor_of = factor_of * jnp.repeat(steps, shape[axis_at] // blocks).reshape([-1 if axis == axis_at else 1 for axis in range(len(shape))])
    return factor_of


def assign_block(rng, own, number, rows, count, top, limit, lean):
    order = jax.random.permutation(rng, count)
    heavy_load, common = shares(count, rows * top, limit, lean, True), shares(count, rows * top, limit, lean, False)
    places = jnp.arange(count)

    def named(sizes, offset_by):
        used = int((sizes > 0).sum())
        fixed = max(1, used // 4)
        passed = fixed + (places - fixed + offset_by * (used - fixed)) % max(1, count - fixed)
        return jnp.zeros((count,), jnp.int32).at[order[jnp.where(places < fixed, places, passed)]].set(jnp.asarray(sizes, jnp.int32))

    sizes = jnp.where(number % 4 == 0, named(heavy_load, number // 4), named(common, number - number // 4 - 1))
    mixed = jax.random.permutation(jax.random.fold_in(own, 3), count)
    giver, sink = mixed[0:count // 2 * 2:2], mixed[1:count // 2 * 2:2]
    slack = jnp.minimum(sizes[giver] - 1, limit - sizes[sink]) // 2
    slack = jnp.where((giver == order[0]) | (sink == order[0]) | (sizes[sink] == 0), 0, jnp.maximum(slack, 0))
    passed = jax.random.randint(jax.random.fold_in(own, 4), (count // 2,), 0, 1 << 20) % (slack + 1)
    sizes = sizes.at[giver].add(-passed).at[sink].add(passed)
    items = jnp.searchsorted(jnp.cumsum(sizes), jnp.arange(rows * top), side="right").astype(jnp.int32)
    grid = items.reshape(top, rows).T
    grid = grid[jax.random.permutation(jax.random.fold_in(own, 1), rows)]
    offset_by = jax.random.randint(jax.random.fold_in(own, 2), (rows, 1), 0, top)
    return jnp.take_along_axis(grid, (jnp.arange(top)[None, :] + offset_by) % top, axis=1)


def shares(amount, total, limit, skew, full):
    loads = [(1 << 20) // math.isqrt(grade ** skew) + 1 for grade in range(1, amount + 1)]
    largest = limit if full else min(limit, max(-(-total // amount), total * loads[0] // sum(loads)))
    least = 1 if total - largest >= amount - 1 else 0
    counts, rest = [largest] + [least] * (amount - 1), total - largest - least * (amount - 1)
    while rest > 0:
        movable = [i for i in range(1, amount) if counts[i] < largest] or [i for i in range(1, amount) if counts[i] < limit]
        mass, remaining = sum([loads[i] for i in movable]), rest
        for i in movable:
            more = min(limit - counts[i], max(1, remaining * loads[i] // mass), rest)
            counts[i] = counts[i] + more
            rest = rest - more
    return np.array(counts)


def normal_values(stream_key, extent, scale, reach, split=(), kind=jnp.bfloat16):
    factor_of = steps_of(stream_key, extent, split, -0.22, 0.18) if split else 1.0
    result = jax.random.normal(stream_key, extent, jnp.float32) * scale * factor_of
    return jnp.minimum(jnp.maximum(result, -reach), reach).astype(kind)


def setup_inputs(seed: int = 0) -> dict:
    streams_of = jax.random.split(jax.random.key(seed), 8)
    tokens = normal_values(streams_of[0], (TOKENS, D), 1.0, 6.0, ((0, 32),))
    cotangent = normal_values(streams_of[1], (TOKENS, D), 1.0, 6.0, ((0, 32),))
    logits = normal_values(streams_of[2], (TOKENS, EXPERTS), 2.0, 8.0, ((0, 32),), jnp.float32)
    expert_ids_keys = jax.random.split(jax.random.fold_in(streams_of[3], 1), TOKENS // TOK_DEV)
    expert_ids_turns = jax.random.permutation(jax.random.fold_in(streams_of[3], 3), TOKENS // TOK_DEV)
    expert_ids = jax.vmap(lambda own, number: assign_block(jax.random.fold_in(streams_of[3], 2), own, number, TOK_DEV, EXPERTS, TOP, CAP, 2))(expert_ids_keys, expert_ids_turns).reshape((TOKENS, TOP))
    gate_proj = normal_values(streams_of[4], (HELD * SPLIT, D, FF_DEV), D ** -0.5, 0.0625, ((0, 16),))
    up_proj = normal_values(streams_of[5], (HELD * SPLIT, D, FF_DEV), D ** -0.5, 0.0625, ((0, 16),))
    down_proj = normal_values(streams_of[6], (HELD * SPLIT, FF_DEV, D), FF ** -0.5, 0.125, ((0, 16),))
    return {"tokens": tokens, "cotangent": cotangent, "logits": logits, "expert_ids": expert_ids, "gate_proj": gate_proj, "up_proj": up_proj, "down_proj": down_proj}


SCALE = 2.5

def slot_ranks(block_ids, experts):
    flat = block_ids.reshape(-1)
    onehot = (flat[:, None] == jnp.arange(experts, dtype=jnp.int32)[None, :]).astype(jnp.int32)
    before = jnp.cumsum(onehot, axis=0) - onehot
    return lax.optimization_barrier(jnp.sum(before * onehot, axis=1)).astype(jnp.int32)

def router_weights(logits, expert_ids):
    experts = logits.shape[1]
    pick = (expert_ids[:, :, None] == jnp.arange(experts, dtype=jnp.int32)[None, None, :]).astype(jnp.float32)
    chosen = lax.optimization_barrier(jnp.sum(pick * jax.nn.sigmoid(logits)[:, None, :], axis=2))
    total = lax.optimization_barrier(jnp.sum(chosen, axis=1, keepdims=True))
    return (pick, chosen, total, SCALE * chosen / total)

def router_grad(pick, chosen, total, dweight):
    inner = lax.optimization_barrier(jnp.sum(dweight * chosen, axis=1, keepdims=True)) / total
    dchosen = SCALE / total * (dweight - inner)
    dlogit = dchosen * chosen * (1.0 - chosen)
    return lax.optimization_barrier(jnp.sum(pick * dlogit[:, :, None], axis=1))

def expert_forward(rows, gate, up):
    gated = jnp.dot(rows, gate, preferred_element_type=jnp.float32)
    upped = jnp.dot(rows, up, preferred_element_type=jnp.float32)
    sig = jax.nn.sigmoid(gated)
    active = gated * sig
    hidden = (active * upped).astype(jnp.bfloat16)
    return (gated, upped, sig, active, hidden)

def expert_backward(forward, cot, weight_b, gate, up, down):
    gated, upped, sig, active, hidden = forward
    contract = (((1,), (1,)), ((), ()))
    proj = lax.dot_general(cot, down, contract, preferred_element_type=jnp.float32)
    dots = lax.optimization_barrier(jnp.sum(hidden.astype(jnp.float32) * proj, axis=1)).astype(jnp.bfloat16)
    dhidden = weight_b.astype(jnp.float32)[:, None] * proj
    dgate = (dhidden * upped * sig * (1.0 + gated * (1.0 - sig))).astype(jnp.bfloat16)
    dup = (dhidden * active).astype(jnp.bfloat16)
    back = lax.dot_general(dgate, gate, contract, preferred_element_type=jnp.float32)
    back = back + lax.dot_general(dup, up, contract, preferred_element_type=jnp.float32)
    scaled = (weight_b.astype(jnp.float32)[:, None] * cot.astype(jnp.float32)).astype(jnp.bfloat16)
    dweight = lax.dot_general(hidden, scaled, (((0,), (0,)), ((), ())), preferred_element_type=jnp.float32)
    return (dots, back.astype(jnp.bfloat16), dweight)

def reference(tokens, cotangent, logits, expert_ids, gate_proj, up_proj, down_proj):
    held = gate_proj.shape[0] // SPLIT
    piece_width = gate_proj.shape[2]
    width = tokens.shape[1]
    experts = logits.shape[1]
    top = expert_ids.shape[1]
    total_tok = tokens.shape[0]
    sources = total_tok // TOK_DEV
    pick, chosen, total, weight = router_weights(logits, expert_ids)
    weight_b = weight.astype(jnp.bfloat16).reshape(-1)
    ranks = lax.map(lambda blk: slot_ranks(blk, experts), expert_ids.reshape(sources, TOK_DEV, top)).reshape(-1)
    flat_ids = expert_ids.reshape(-1)
    entry = jnp.arange(total_tok * top, dtype=jnp.int32)
    source = entry // (TOK_DEV * top)
    inside = flat_ids < held
    target = jnp.where(inside, flat_ids, held).astype(jnp.int32)
    column = (source * CAP + ranks).astype(jnp.int32)
    table = jnp.full((held, sources * CAP), -1, jnp.int32).at[target, column].set(entry, mode='drop')
    gates = gate_proj.reshape(held, SPLIT, width, piece_width)
    ups = up_proj.reshape(held, SPLIT, width, piece_width)
    downs = down_proj.reshape(held, SPLIT, piece_width, width)

    def one_expert(carry, inputs):
        back_sum, dots_all = carry
        slots, gate_e, up_e, down_e = inputs
        live = slots >= 0
        entry_safe = jnp.where(live, slots, 0).astype(jnp.int32)
        tok = (entry_safe // top).astype(jnp.int32)
        rows = jnp.where(live[:, None], tokens[tok], jnp.zeros((), jnp.bfloat16))
        cot = jnp.where(live[:, None], cotangent[tok], jnp.zeros((), jnp.bfloat16))
        wsl = jnp.where(live, weight_b[entry_safe], jnp.zeros((), jnp.bfloat16))

        def one_piece(acc, pieces):
            back_acc, dots_acc = acc
            gate, up, down = pieces
            forward = expert_forward(rows, gate, up)
            dots, back, dweight = expert_backward(forward, cot, wsl, gate, up, down)
            return ((back_acc + back.astype(jnp.float32), dots_acc + dots.astype(jnp.float32)), dweight.astype(jnp.bfloat16))
        start_acc = (jnp.zeros(rows.shape, jnp.float32), jnp.zeros((rows.shape[0],), jnp.float32))
        (back_acc, dots_acc), piece_grads = lax.scan(one_piece, start_acc, (gate_e, up_e, down_e))
        back_sum = back_sum.at[tok].add(jnp.where(live[:, None], back_acc, jnp.zeros((), jnp.float32)))
        dots_all = dots_all.at[entry_safe].add(jnp.where(live, dots_acc, jnp.zeros((), jnp.float32)))
        return ((back_sum, dots_all), piece_grads)
    start = (jnp.zeros((total_tok, width), jnp.float32), jnp.zeros((total_tok * top,), jnp.float32))
    (back_sum, dots_all), down_grad = lax.scan(one_expert, start, (table, gates, ups, downs))
    dweight_tk = jnp.where(inside, dots_all, jnp.zeros((), jnp.float32)).reshape(total_tok, top)
    logit_grad = router_grad(pick, chosen, total, dweight_tk)
    return (back_sum.astype(jnp.bfloat16), logit_grad, down_grad.reshape(held * SPLIT, piece_width, width))
```

```python
import jax
import jax.numpy as jnp
from jax import lax
from jax.sharding import PartitionSpec as P

SPLIT = 16
SCALE = 2.5
PAIR = 2


def router(logits, expert_ids):
    experts = logits.shape[1]
    lane = jnp.arange(experts, dtype=jnp.int32)[None, None, :]
    has = jnp.any(expert_ids[:, :, None] == lane, axis=1)
    chosen = jnp.where(has, jax.nn.sigmoid(logits), 0.0)
    total = jnp.sum(chosen, axis=1, keepdims=True)
    return has, chosen, total, SCALE * chosen / total


def select_matrix(has, held, capacity):
    count = has.shape[0]
    live = has[:, :held]
    row = jnp.arange(count, dtype=jnp.int32)
    before = (row[None, :] < row[:, None]).astype(jnp.bfloat16)
    rank = jnp.dot(before, live.astype(jnp.bfloat16), preferred_element_type=jnp.float32)
    slot = jnp.arange(capacity, dtype=jnp.float32)
    pick = live[:, :, None] & (rank[:, :, None] == slot[None, None, :])
    return pick.astype(jnp.bfloat16)


def per_device(tokens, cotangent, logits, expert_ids, gate_proj, up_proj, down_proj):
    devices = lax.axis_size("expert")
    cores = lax.axis_size("dp")
    core = lax.axis_index("dp")
    held = devices // SPLIT
    tok_count, top = expert_ids.shape
    experts = logits.shape[1]
    width = tokens.shape[1]
    capacity = max(2, 5 * tok_count * top // (4 * experts))
    members = SPLIT // PAIR
    index = lax.axis_index("expert")
    across = [[e * SPLIT + j for e in range(held)] for j in range(SPLIT)]
    within = [
        [e * SPLIT + m * PAIR + p for m in range(members)] for e in range(held) for p in range(PAIR)
    ]
    swap = [(i, i ^ 1) for i in range(devices)]

    part = width // cores
    gate, up, down = gate_proj[0], up_proj[0], down_proj[0]
    send_w = jnp.concatenate(
        [
            lax.dynamic_slice_in_dim(gate, core * part, part, 0),
            lax.dynamic_slice_in_dim(up, core * part, part, 0),
        ],
        axis=1,
    )
    send_d = lax.dynamic_slice_in_dim(down, core * part, part, 1)
    got_w = lax.ppermute(send_w, "expert", swap)
    got_d = lax.ppermute(send_d, "expert", swap)
    pair_w = lax.all_gather(got_w, "dp", axis=0, tiled=True)
    pair_d = lax.all_gather(got_d, "dp", axis=0, tiled=False)
    pair_d = jnp.transpose(pair_d, (1, 0, 2)).reshape(down.shape)

    has, chosen, total, weight = router(logits, expert_ids)
    weight_b = weight[:, :held].astype(jnp.bfloat16)
    pick = select_matrix(has, held, capacity)
    pick2 = pick.reshape(tok_count, held * capacity)
    contract0 = (((0,), (0,)), ((), ()))
    rows = lax.dot_general(pick2, tokens, contract0, preferred_element_type=jnp.float32)
    cots = lax.dot_general(pick2, cotangent, contract0, preferred_element_type=jnp.float32)
    slot_w = jnp.sum(
        pick.astype(jnp.float32) * weight_b.astype(jnp.float32)[:, :, None], axis=0
    ).reshape(held * capacity, 1)
    rows = rows.astype(jnp.bfloat16).reshape(held, capacity, width)
    scaled = (cots * slot_w).astype(jnp.bfloat16).reshape(held, capacity, width)

    def gather(block):
        if held > 1:
            block = lax.all_to_all(
                block, "expert", 0, 0, axis_index_groups=across, tiled=True
            )
        full = lax.all_gather(block, "expert", axis_index_groups=within, axis=0, tiled=True)
        return full.reshape(members * held * capacity, width)

    x = gather(rows)
    sc = gather(scaled)

    gu_w = jnp.concatenate([gate, up], axis=1)
    ff = gate.shape[1]
    own = jnp.dot(x, gu_w, preferred_element_type=jnp.float32)
    oth = jnp.dot(x, pair_w, preferred_element_type=jnp.float32)
    g = jnp.concatenate([own[:, :ff], oth[:, :ff]], axis=1)
    u = jnp.concatenate([own[:, ff:], oth[:, ff:]], axis=1)
    contract = (((1,), (1,)), ((), ()))
    dn = jnp.concatenate([down, pair_d], axis=0)
    proj = lax.dot_general(sc, dn, contract, preferred_element_type=jnp.float32)
    sig = jax.nn.sigmoid(g)
    active = g * sig
    hidden = (active * u).astype(jnp.bfloat16)
    dots = jnp.sum(hidden.astype(jnp.float32) * proj, axis=1)
    dgate = (proj * u * sig * (1.0 + g * (1.0 - sig))).astype(jnp.bfloat16)
    dup = (proj * active).astype(jnp.bfloat16)
    d_own = jnp.concatenate([dgate[:, :ff], dup[:, :ff]], axis=1)
    d_oth = jnp.concatenate([dgate[:, ff:], dup[:, ff:]], axis=1)
    back = lax.dot_general(d_own, gu_w, contract, preferred_element_type=jnp.float32)
    back = back + lax.dot_general(d_oth, pair_w, contract, preferred_element_type=jnp.float32)
    back = back.astype(jnp.bfloat16)

    dots_all = lax.all_gather(dots, "expert", axis_index_groups=within, axis=0)
    back_sum = lax.psum_scatter(
        back.reshape(members * held, capacity, width),
        "expert",
        scatter_dimension=0,
        axis_index_groups=within,
        tiled=True,
    )
    member = (index % SPLIT) // PAIR
    dots_sum = jnp.sum(dots_all, axis=0).reshape(members, held, capacity)
    dots_mine = lax.dynamic_index_in_dim(dots_sum, member, 0, keepdims=False)
    if held > 1:
        back_sum = lax.all_to_all(
            back_sum, "expert", 0, 0, axis_index_groups=across, tiled=True
        )
        dots_mine = lax.all_to_all(
            dots_mine, "expert", 0, 0, axis_index_groups=across, tiled=True
        )
    grad_d = lax.dot_general(hidden, sc, contract0, preferred_element_type=jnp.float32)
    grad_part = lax.psum_scatter(
        grad_d.astype(jnp.bfloat16), "dp", scatter_dimension=1, tiled=True
    )
    grad_got = lax.ppermute(grad_part[ff:], "expert", swap)
    down_grad = (grad_part[:ff].astype(jnp.float32) + grad_got.astype(jnp.float32)).astype(
        jnp.bfloat16
    )[None]

    token_grad = jnp.dot(
        pick2, back_sum.reshape(held * capacity, width), preferred_element_type=jnp.float32
    ).astype(jnp.bfloat16)
    dw = jnp.sum(pick.astype(jnp.float32) * dots_mine[None], axis=2)
    live = has[:, :held]
    dw = jnp.where(live, dw / jnp.where(live, weight_b.astype(jnp.float32), 1.0), 0.0)
    dw = jnp.pad(dw, ((0, 0), (0, experts - held)))
    inner = jnp.sum(dw * chosen, axis=1, keepdims=True) / total
    dchosen = SCALE / total * (dw - inner)
    logit_grad = jnp.where(has, dchosen * chosen * (1.0 - chosen), 0.0)
    return (token_grad, logit_grad, down_grad)


def solution(mesh):
    in_specs = (
        P(("expert", "dp"), None),
        P(("expert", "dp"), None),
        P(("expert", "dp"), None),
        P(("expert", "dp"), None),
        P("expert", None, None),
        P("expert", None, None),
        P("expert", None, None),
    )
    out_specs = (P(("expert", "dp"), None), P(("expert", "dp"), None), P("expert", None, "dp"))
    return jax.shard_map(
        per_device, mesh=mesh, in_specs=in_specs, out_specs=out_specs, check_vma=False
    )
```

```python
import jax
import jax.numpy as jnp
from jax import lax
from jax.sharding import PartitionSpec as P

SPLIT = 16
SCALE = 2.5
QUAD = 4
bf16 = jnp.bfloat16
f32 = jnp.float32
CONTRACT0 = (((0,), (0,)), ((), ()))
CONTRACT1 = (((1,), (1,)), ((), ()))


def router(logits, expert_ids):
    experts = logits.shape[1]
    lane = jnp.arange(experts, dtype=jnp.int32)[None, None, :]
    has = jnp.any(expert_ids[:, :, None] == lane, axis=1)
    chosen = jnp.where(has, jax.nn.sigmoid(logits), 0.0)
    total = jnp.sum(chosen, axis=1, keepdims=True)
    return has, chosen, total, SCALE * chosen / total


def select_matrix(has, held, capacity):
    count = has.shape[0]
    live = has[:, :held]
    row = jnp.arange(count, dtype=jnp.int32)
    before = (row[None, :] < row[:, None]).astype(bf16)
    rank = jnp.dot(before, live.astype(bf16), preferred_element_type=f32)
    slot = jnp.arange(capacity, dtype=f32)
    pick = live[:, :, None] & (rank[:, :, None] == slot[None, None, :])
    return pick.astype(bf16)


def per_device(tokens, cotangent, logits, expert_ids, gate_proj, up_proj, down_proj):
    devices = lax.axis_size("expert")
    cores = lax.axis_size("dp")
    core = lax.axis_index("dp")
    index = lax.axis_index("expert")
    held = devices // SPLIT
    tok_count, top = expert_ids.shape
    experts = logits.shape[1]
    width = tokens.shape[1]
    ff = gate_proj.shape[2]
    part = width // cores
    capacity = max(2, 5 * tok_count * top // (4 * experts))
    members = SPLIT // QUAD
    member = (index % SPLIT) // QUAD
    across = [[e * SPLIT + j for e in range(held)] for j in range(SPLIT)]
    within = [
        [e * SPLIT + m * QUAD + q for m in range(members)] for e in range(held) for q in range(QUAD)
    ]
    swap1 = [(i, i ^ 1) for i in range(devices)]
    swap2 = [(i, i ^ 2) for i in range(devices)]
    cross = [(i, i ^ 3) for i in range(devices)]
    sibling = [(c, cores - 1 - c) for c in range(cores)]

    gu0 = jnp.concatenate(
        [
            lax.dynamic_slice_in_dim(gate_proj[0], core * part, part, 0),
            lax.dynamic_slice_in_dim(up_proj[0], core * part, part, 0),
        ],
        axis=1,
    )
    dn0 = lax.dynamic_slice_in_dim(down_proj[0], core * part, part, 1)
    gu0, logits, tokens = lax.optimization_barrier((gu0, logits, tokens))
    gu1 = lax.ppermute(gu0, "expert", swap1)
    gu2 = lax.ppermute(gu0, "expert", swap2)

    has, chosen, total, weight = router(logits, expert_ids)
    weight_b = weight[:, :held].astype(bf16)
    pick = select_matrix(has, held, capacity)
    pick2 = pick.reshape(tok_count, held * capacity)
    slot_w = jnp.sum(pick.astype(f32) * weight_b.astype(f32)[:, :, None], axis=0).reshape(
        held * capacity, 1
    )

    def halves(array):
        mine = lax.dynamic_slice_in_dim(array, core * part, part, 1)
        other = lax.dynamic_slice_in_dim(array, (cores - 1 - core) * part, part, 1)
        return mine, other

    def join(mine, theirs):
        first = jnp.where(core == 0, mine, theirs)
        second = jnp.where(core == 0, theirs, mine)
        return jnp.stack([first, second], axis=1)

    rows = lax.dot_general(pick2, tokens, CONTRACT0, preferred_element_type=f32).astype(bf16)
    cots = lax.dot_general(pick2, cotangent, CONTRACT0, preferred_element_type=f32)
    scaled = (cots * slot_w).astype(bf16)

    def spread(array):
        mine, other = halves(array)
        theirs = lax.ppermute(other, "dp", sibling)
        shape = (held, capacity, part)
        return join(mine.reshape(shape), theirs.reshape(shape))

    def gather(block):
        if held > 1:
            block = lax.all_to_all(block, "expert", 0, 0, axis_index_groups=across, tiled=True)
        block = block.reshape(held * cores * capacity, part)
        return lax.all_gather(block, "expert", axis_index_groups=within, axis=0, tiled=True)

    x_block, s_block = spread(rows), spread(scaled)
    x = gather(x_block)
    sc = gather(s_block)

    dn0, x_block = lax.optimization_barrier((dn0, x_block))
    dn1 = lax.ppermute(dn0, "expert", swap1)
    dn2 = lax.ppermute(dn0, "expert", swap2)
    low, lowf = part // 2, ff // 2
    gu3a = lax.ppermute(gu2[:low], "expert", swap1)
    gu3b = lax.ppermute(gu1[low:], "expert", swap2)
    dn3a = lax.ppermute(dn2[:lowf], "expert", swap1)
    dn3b = lax.ppermute(dn1[lowf:], "expert", swap2)

    def add_sibling(array):
        return array + lax.ppermute(array, "dp", sibling)

    dot = lambda a, b: jnp.dot(a, b, preferred_element_type=f32)
    dot1 = lambda a, b: lax.dot_general(a, b, CONTRACT1, preferred_element_type=f32)
    gu3 = jnp.concatenate([gu3a, gu3b], axis=0)
    dn3 = jnp.concatenate([dn3a, dn3b], axis=0)
    packs = (gu0, gu1, gu2, gu3)
    products = [dot(x, w) for w in packs]
    g_u = add_sibling(
        jnp.concatenate([p[:, :ff] for p in products] + [p[:, ff:] for p in products], axis=1)
    )
    proj = add_sibling(jnp.concatenate([dot1(sc, w) for w in (dn0, dn1, dn2, dn3)], axis=1))
    g, u = g_u[:, : QUAD * ff], g_u[:, QUAD * ff :]
    sig = jax.nn.sigmoid(g)
    active = g * sig
    hidden = (active * u).astype(bf16)
    dots = jnp.sum(hidden.astype(f32) * proj, axis=1)
    dgate = (proj * u * sig * (1.0 + g * (1.0 - sig))).astype(bf16)
    dup = (proj * active).astype(bf16)
    d_gu = jnp.concatenate([dgate, dup], axis=1)
    w_gu = jnp.concatenate([w[:, :ff] for w in packs] + [w[:, ff:] for w in packs], axis=1)
    back = dot1(d_gu, w_gu).astype(bf16)
    back_sum = lax.psum_scatter(
        back.reshape(members, held * cores * capacity, part),
        "expert",
        scatter_dimension=0,
        axis_index_groups=within,
        tiled=True,
    ).reshape(held, cores, capacity, part)

    grads = lax.dot_general(
        hidden, sc, CONTRACT0, preferred_element_type=f32
    ).astype(bf16)
    parts = [grads[:ff]] + [
        lax.ppermute(grads[q * ff : (q + 1) * ff], "expert", route)
        for q, route in ((1, swap1), (2, swap2), (3, cross))
    ]
    down_grad = sum(p.astype(f32) for p in parts).astype(bf16)[None]

    dots = dots.reshape(members, held * cores * capacity)
    dots_mine = lax.dynamic_index_in_dim(dots, member, 0, keepdims=False)
    for shift in range(1, members):
        target = lax.rem(member + shift, members)
        route = [
            (e * SPLIT + m * QUAD + q, e * SPLIT + (m + shift) % members * QUAD + q)
            for e in range(held)
            for m in range(members)
            for q in range(QUAD)
        ]
        sent = lax.dynamic_index_in_dim(dots, target, 0, keepdims=False)
        dots_mine = dots_mine + lax.ppermute(sent, "expert", route)
    dots_mine = dots_mine.reshape(held, cores, capacity)

    if held > 1:
        back_sum = lax.all_to_all(back_sum, "expert", 0, 0, axis_index_groups=across, tiled=True)
        dots_mine = lax.all_to_all(dots_mine, "expert", 0, 0, axis_index_groups=across, tiled=True)
    dots_mine = lax.dynamic_index_in_dim(dots_mine, core, 1, keepdims=False)
    mine = lax.dynamic_index_in_dim(back_sum, core, 1, keepdims=False)
    other = lax.dynamic_index_in_dim(back_sum, cores - 1 - core, 1, keepdims=False)
    theirs = lax.ppermute(other, "dp", sibling)
    shape = (held * capacity, part)
    gm, gt = dot(pick2, mine.reshape(shape)), dot(pick2, theirs.reshape(shape))
    token_grad = jnp.concatenate(
        [jnp.where(core == 0, gm, gt), jnp.where(core == 0, gt, gm)], axis=1
    ).astype(bf16)
    dw = jnp.sum(pick.astype(f32) * dots_mine[None], axis=2)
    live = has[:, :held]
    dw = jnp.where(live, dw / jnp.where(live, weight_b.astype(f32), 1.0), 0.0)
    dw = jnp.pad(dw, ((0, 0), (0, experts - held)))
    inner = jnp.sum(dw * chosen, axis=1, keepdims=True) / total
    dchosen = SCALE / total * (dw - inner)
    logit_grad = jnp.where(has, dchosen * chosen * (1.0 - chosen), 0.0)
    return (token_grad, logit_grad, down_grad)


def solution(mesh):
    in_specs = (
        P(("expert", "dp"), None),
        P(("expert", "dp"), None),
        P(("expert", "dp"), None),
        P(("expert", "dp"), None),
        P("expert", None, None),
        P("expert", None, None),
        P("expert", None, None),
    )
    out_specs = (P(("expert", "dp"), None), P(("expert", "dp"), None), P("expert", None, "dp"))
    return jax.shard_map(
        per_device, mesh=mesh, in_specs=in_specs, out_specs=out_specs, check_vma=False
    )
```

```python
import jax
import jax.numpy as jnp
from jax import lax
from jax.experimental import pallas as pl
from jax.experimental.pallas import tpu as pltpu
from jax.sharding import PartitionSpec as P

SPLIT = 16
SCALE = 2.5
QUAD = 4
bf16 = jnp.bfloat16
f32 = jnp.float32
CONTRACT0 = (((0,), (0,)), ((), ()))
CONTRACT1 = (((1,), (1,)), ((), ()))
VMEM = pl.BlockSpec(memory_space=pltpu.VMEM)


def chunk_of(size, limit):
    best = 128
    for step in range(128, limit + 1, 128):
        if size % step == 0:
            best = step
    return best


def slot_rows(blocks, first, count, columns):
    member = lax.rem(lax.axis_index("expert"), SPLIT) // QUAD
    own, far, up, down, end = [b[first : first + count, columns] for b in blocks]
    below = jnp.where(member == 0, end, up)
    above = jnp.where(member == SPLIT // QUAD - 1, end, down)
    return jnp.concatenate([own, far, below, above], axis=0)


def prep_kernel(held, capacity, *refs):
    gate, up, down, tokens, cotangent, logits, ids = refs[:7]
    gu_top, gu_low, dn_top, dn_low, mine, other, pick_out = refs[7:14]
    chosen_out, inv_w_out, inv_total_out, sems = refs[14:]
    half, wide = gu_top.shape
    ff = wide // 2
    rows, part = dn_top.shape
    core = lax.axis_index("dp")
    start = pl.multiple_of(core * part, 128)
    away = pl.multiple_of((1 - core) * part, 128)
    copies = []
    for side, (gu, dn) in enumerate(((gu_top, dn_top), (gu_low, dn_low))):
        at = pl.ds(pl.multiple_of(start + side * half, 128), half)
        pairs = (
            (gate.at[0, at, :], gu.at[:, :ff]),
            (up.at[0, at, :], gu.at[:, ff:]),
            (down.at[0, side * rows : (side + 1) * rows, pl.ds(start, part)], dn),
        )
        for i, (src, dst) in enumerate(pairs):
            copies.append(pltpu.make_async_copy(src, dst, sems.at[3 * side + i]))
    for copy in copies:
        copy.start()

    experts, count = logits.shape
    expert = lax.broadcasted_iota(jnp.int32, (experts, count), 0)
    has = expert == ids[0:1, :]
    for k in range(1, ids.shape[0]):
        has = has | (expert == ids[k : k + 1, :])
    chosen = jnp.where(has, jax.nn.sigmoid(logits[...]), 0.0)
    total = jnp.sum(chosen, axis=0, keepdims=True)
    weight = (SCALE * chosen / total).astype(bf16).astype(f32)
    before = lax.broadcasted_iota(jnp.int32, (count, count), 0)
    after = lax.broadcasted_iota(jnp.int32, (count, count), 1)
    earlier = jnp.where(before < after, 1.0, 0.0).astype(bf16)
    named = jnp.where(has, 1.0, 0.0)
    rank = jnp.dot(named.astype(bf16), earlier, preferred_element_type=f32)
    slots = held * capacity
    slot = lax.broadcasted_iota(jnp.int32, (slots, count), 0)
    pick = jnp.zeros((slots, count), f32)
    value = jnp.zeros((slots, count), f32)
    for e in range(held):
        place = rank[e : e + 1, :].astype(jnp.int32) + e * capacity
        hit = jnp.where(slot == place, named[e : e + 1, :], 0.0)
        pick = pick + hit
        value = value + hit * weight[e : e + 1, :]
    value = jnp.sum(value, axis=1, keepdims=True)
    pick = pick.astype(bf16)
    pick_out[...] = pick
    chosen_out[...] = chosen
    inv_w_out[...] = jnp.where(has & (expert < held), 1.0 / weight, 0.0)
    inv_total_out[...] = jnp.broadcast_to(1.0 / total, chosen.shape)

    step = chunk_of(part, 512)

    def body(k, carry):
        at = pl.multiple_of(k * step, 128)
        for base, out in ((start, mine), (away, other)):
            columns = pl.ds(pl.multiple_of(base + at, 128), step)
            x = jnp.dot(pick, tokens[:, columns], preferred_element_type=f32)
            c = jnp.dot(pick, cotangent[:, columns], preferred_element_type=f32)
            out[0, :, pl.ds(at, step)] = x.astype(bf16)
            out[1, :, pl.ds(at, step)] = (c * value).astype(bf16)
        return carry

    lax.fori_loop(0, part // step, body, 0)
    for copy in copies:
        copy.wait()


def sum_kernel(own, above, below, far, mine, other, tail):
    first = lax.axis_index("dp") == 0
    rows, part = mine.shape
    step = chunk_of(part, 512)

    def total(columns):
        value = own[:, columns].astype(f32) + above[:, columns].astype(f32)
        value = value + below[:, columns].astype(f32) + far[:, columns].astype(f32)
        top, low = value[:rows], value[rows:]
        return jnp.where(first, top, low), jnp.where(first, low, top)

    def body(k, carry):
        columns = pl.ds(pl.multiple_of(k * step, 128), step)
        here, there = total(columns)
        mine[:, columns] = here.astype(bf16)
        other[:, columns] = there.astype(bf16)
        return carry

    lax.fori_loop(0, part // step, body, 0)
    tail[...] = total(slice(part, part + 128))[0]


def gate_up_kernel(*refs):
    blocks, packs, out = refs[:5], refs[5:-1], refs[-1]
    half, wide = packs[0].shape
    count = out.shape[0] // (SPLIT // QUAD)
    step = chunk_of(half, 1024)
    out[...] = jnp.zeros_like(out)
    for side in range(2):

        def body(k, carry):
            at = pl.multiple_of(k * step, 128)
            columns = pl.ds(pl.multiple_of(side * half + k * step, 128), step)
            x = slot_rows(blocks, 0, count, columns)
            for q in range(QUAD):
                w = packs[2 * q + side][pl.ds(at, step), :]
                out[:, q * wide : (q + 1) * wide] += jnp.dot(x, w, preferred_element_type=f32)
            return carry

        lax.fori_loop(0, half // step, body, 0)


def proj_kernel(*refs):
    blocks, packs, out = refs[:5], refs[5:-1], refs[-1]
    part = packs[0].shape[1]
    count = out.shape[0] // (SPLIT // QUAD)
    step = chunk_of(part, 1024)
    out[...] = jnp.zeros_like(out)

    def body(k, carry):
        columns = pl.ds(pl.multiple_of(k * step, 128), step)
        rows = slot_rows(blocks, count, count, columns)
        w = jnp.concatenate([p[:, columns] for p in packs], axis=0)
        out[...] += lax.dot_general(rows, w, CONTRACT1, preferred_element_type=f32)
        return carry

    lax.fori_loop(0, part // step, body, 0)


def activations(mine, theirs, q, ff):
    base = 2 * q * ff
    g = mine[:, base : base + ff] + theirs[:, base : base + ff]
    u = mine[:, base + ff : base + 2 * ff] + theirs[:, base + ff : base + 2 * ff]
    sig = jax.nn.sigmoid(g)
    return g, u, sig, g * sig


def down_kernel(mine, theirs, *refs):
    blocks, outs, scratch = refs[:5], refs[5:-1], refs[-1]
    ff, part = outs[0].shape
    count = scratch.shape[1] // (SPLIT // QUAD)
    step = chunk_of(part, 512)
    for q in range(QUAD):
        g, u, sig, active = activations(mine, theirs, q, ff)
        hidden = (active * u).astype(bf16).astype(f32)
        scratch[q * ff : (q + 1) * ff, :] = hidden.T.astype(bf16)

    def body(k, carry):
        columns = pl.ds(pl.multiple_of(k * step, 128), step)
        rows = slot_rows(blocks, count, count, columns)
        grads = jnp.dot(scratch[...], rows, preferred_element_type=f32).astype(bf16)
        at = 0
        for out in outs:
            out[:, columns] = grads[at : at + out.shape[0]]
            at += out.shape[0]
        return carry

    lax.fori_loop(0, part // step, body, 0)


def back_kernel(mine, theirs, proj_mine, proj_theirs, *refs):
    packs, outs, scratch = refs[: 2 * QUAD], refs[2 * QUAD : -1], refs[-1]
    half, wide = packs[0].shape
    ff = wide // 2
    rows = outs[0].shape[0]
    step = chunk_of(half, 256)
    dots = 0.0
    for q in range(QUAD):
        g, u, sig, active = activations(mine, theirs, q, ff)
        proj = proj_mine[:, q * ff : (q + 1) * ff] + proj_theirs[:, q * ff : (q + 1) * ff]
        hidden = (active * u).astype(bf16).astype(f32)
        dots = dots + jnp.sum(hidden * proj, axis=1, keepdims=True)
        base = 2 * q * ff
        scratch[:, base : base + ff] = (proj * u * sig * (1.0 + g * (1.0 - sig))).astype(bf16)
        scratch[:, base + ff : base + 2 * ff] = (proj * active).astype(bf16)

    def write(values, columns):
        for i, out in enumerate(outs):
            out[:, columns] = values[i * rows : (i + 1) * rows].astype(bf16)

    high = dots.astype(bf16).astype(f32)
    rest = dots - high
    lane = lax.broadcasted_iota(jnp.int32, (dots.shape[0], 128), 1)
    tail = slice(2 * half, 2 * half + 128)
    write(jnp.where(lane == 0, high, jnp.where(lane == 1, rest, 0.0)), tail)
    for side in range(2):

        def body(k, carry):
            at = pl.multiple_of(k * step, 128)
            columns = pl.ds(pl.multiple_of(side * half + k * step, 128), step)
            w = jnp.concatenate(
                [packs[2 * q + side][pl.ds(at, step), :] for q in range(QUAD)], axis=1
            )
            grads = lax.dot_general(scratch[...], w, CONTRACT1, preferred_element_type=f32)
            write(grads, columns)
            return carry

        lax.fori_loop(0, half // step, body, 0)


def final_kernel(held, pick, mine, theirs, tail, chosen, inv_w, inv_total, tok_out, logit_out):
    core = lax.axis_index("dp")
    slots, part = mine.shape
    step = chunk_of(part, 512)
    pick_t = pick[...]

    def body(k, carry):
        at = pl.multiple_of(k * step, 128)
        for source, side in ((mine, core), (theirs, 1 - core)):
            block = lax.dot_general(
                pick_t, source[:, pl.ds(at, step)], CONTRACT0, preferred_element_type=f32
            )
            tok_out[:, pl.ds(pl.multiple_of(side * part + at, 128), step)] = block.astype(bf16)
        return carry

    lax.fori_loop(0, part // step, body, 0)
    values = jnp.sum(tail[...], axis=1, keepdims=True)
    entries = pick_t.astype(f32) * values
    full = chosen.shape
    expert = lax.broadcasted_iota(jnp.int32, full, 0)
    slot = lax.broadcasted_iota(jnp.int32, entries.shape, 0)
    capacity = slots // held
    dw = jnp.zeros(full, f32)
    for e in range(held):
        inside = (slot >= e * capacity) & (slot < (e + 1) * capacity)
        found = jnp.sum(jnp.where(inside, entries, 0.0), axis=0, keepdims=True)
        dw = jnp.where(expert == e, jnp.broadcast_to(found, full), dw)
    dw = dw * inv_w[...]
    share = chosen[...]
    inner = jnp.sum(dw * share, axis=0, keepdims=True) * inv_total[...]
    logit_out[...] = SCALE * inv_total[...] * (dw - inner) * share * (1.0 - share)


def call(kernel, outs, in_specs, scratch, flops, moved, limit=40):
    return pl.pallas_call(
        kernel,
        out_shape=outs,
        in_specs=in_specs,
        out_specs=[VMEM] * len(outs),
        scratch_shapes=scratch,
        compiler_params=pltpu.CompilerParams(vmem_limit_bytes=limit * 1024 * 1024),
        cost_estimate=pl.CostEstimate(flops=flops, bytes_accessed=moved, transcendentals=0),
    )


def per_device(tokens, cotangent, logits, expert_ids, gate_proj, up_proj, down_proj):
    devices = lax.axis_size("expert")
    cores = lax.axis_size("dp")
    core = lax.axis_index("dp")
    held = devices // SPLIT
    tok_count, top = expert_ids.shape
    experts = logits.shape[1]
    width = tokens.shape[1]
    ff = gate_proj.shape[2]
    part = width // cores
    capacity = max(2, 5 * tok_count * top // (4 * experts))
    members = SPLIT // QUAD
    last = members - 1
    rows_dev = held * capacity
    rows_chip = cores * rows_dev
    slots = members * rows_chip
    across = [[e * SPLIT + j for e in range(held)] for j in range(SPLIT)]
    swap1 = [(i, i ^ 1) for i in range(devices)]
    swap2 = [(i, i ^ 2) for i in range(devices)]
    sibling = [(c, cores - 1 - c) for c in range(cores)]
    barrier = lax.optimization_barrier

    def send(array, route):
        return lax.ppermute(array, "expert", route)

    def line(pairs):
        return [
            (e * SPLIT + a * QUAD + q, e * SPLIT + b * QUAD + q)
            for e in range(held)
            for a, b in pairs
            for q in range(QUAD)
        ]

    upward = line([(m, m + 1) for m in range(last)])
    downward = line([(m + 1, m) for m in range(last)])
    distant = line([(m, m ^ 2) for m in range(members)])

    low, lowf = part // 2, ff // 2
    shape = jax.ShapeDtypeStruct
    gu_t, gu_b, dn_t, dn_b, mine, other, pick, chosen, inv_w, inv_total = call(
        lambda *refs: prep_kernel(held, capacity, *refs),
        [shape((low, 2 * ff), bf16)] * 2
        + [shape((lowf, part), bf16)] * 2
        + [shape((2, rows_dev, part), bf16)] * 2
        + [shape((rows_dev, tok_count), bf16)]
        + [shape((experts, tok_count), f32)] * 3,
        [pl.BlockSpec(memory_space=pltpu.HBM)] * 3 + [VMEM] * 4,
        [pltpu.SemaphoreType.DMA((6,))],
        4 * rows_dev * tok_count * width,
        12 * part * ff + 4 * tok_count * width,
        limit=58,
    )(gate_proj, up_proj, down_proj, tokens, cotangent, logits.T, expert_ids.T)
    gu1b = send(gu_b, swap1)
    gu2t = send(gu_t, swap2)

    theirs = lax.ppermute(other, "dp", sibling)
    own = jnp.concatenate(
        [
            jnp.where(core == (0 if side == 0 else cores - 1), mine[i], theirs[i])
            for i in range(2)
            for side in range(cores)
        ],
        axis=0,
    )
    if held > 1:
        own = own.reshape(2, cores, held, capacity, part)
        own = lax.all_to_all(own, "expert", 2, 2, axis_index_groups=across, tiled=True)
        own = own.reshape(2 * rows_chip, part)
    far = send(own, distant)
    up = send(own, upward)
    down = send(own, downward)

    gu_t, gu_b, gu1b, gu2t, own = barrier((gu_t, gu_b, gu1b, gu2t, own))
    gu1t = send(gu_t, swap1)
    gu2b = send(gu_b, swap2)
    gu1b, gu2t, gu1t, gu2b = barrier((gu1b, gu2t, gu1t, gu2b))
    gu3t = send(gu2t, swap1)
    gu3b = send(gu1b, swap2)
    end = send(far, line([(2, 3), (1, 0)]))
    dn_t, dn_b, gu3t, gu3b = barrier((dn_t, dn_b, gu3t, gu3b))
    dn1b = send(dn_b, swap1)
    dn2t = send(dn_t, swap2)
    dn_t, dn_b, dn1b, dn2t = barrier((dn_t, dn_b, dn1b, dn2t))
    dn1t = send(dn_t, swap1)
    dn2b = send(dn_b, swap2)
    dn3t = send(dn2t, swap1)
    dn3b = send(dn1b, swap2)
    gu = [gu_t, gu_b, gu1t, gu1b, gu2t, gu2b, gu3t, gu3b]
    dn = [dn_t, dn_b, dn1t, dn1b, dn2t, dn2b, dn3t, dn3b]
    blocks = [own, far, up, down, end]

    matmul = 2 * slots * part * QUAD * ff
    (g_u,) = call(
        gate_up_kernel,
        [shape((slots, QUAD * 2 * ff), f32)],
        [VMEM] * 13,
        [],
        2 * matmul,
        2 * part * (slots + QUAD * 2 * ff),
    )(*blocks, *gu)
    g_u_sib = lax.ppermute(g_u, "dp", sibling)
    (proj,) = call(
        proj_kernel,
        [shape((slots, QUAD * ff), f32)],
        [VMEM] * 13,
        [],
        matmul,
        2 * part * (slots + QUAD * ff),
    )(*blocks, *dn)
    proj_sib = lax.ppermute(proj, "dp", sibling)
    g0, g1, g2, g3a, g3b = call(
        down_kernel,
        [shape((ff, part), bf16)] * 3
        + [shape((lowf, part), bf16)] * 2,
        [VMEM] * 7,
        [pltpu.VMEM((QUAD * ff, slots), bf16)],
        matmul,
        2 * part * (slots + QUAD * ff),
    )(g_u, g_u_sib, *blocks)
    g0, g3a, g3b, proj, proj_sib = barrier((g0, g3a, g3b, proj, proj_sib))
    r3a = send(g3a, swap1)
    r3b = send(g3b, swap2)
    b0, b1, b2, b3 = call(
        back_kernel,
        [shape((rows_chip, part + 128), bf16)] * members,
        [VMEM] * 12,
        [pltpu.VMEM((slots, QUAD * 2 * ff), bf16)],
        2 * matmul,
        2 * part * (slots + QUAD * 2 * ff),
    )(g_u, g_u_sib, proj, proj_sib, *gu)

    from_above = send(b2, line([(m, (m - 1) % members) for m in range(members)]))
    from_below = send(b3, line([(m, (m + 1) % members) for m in range(members)]))
    from_far = send(b1, distant)

    from_above, r3a, r3b = barrier((from_above, r3a, r3b))
    r1 = send(jnp.concatenate([g1[:lowf], g1[lowf:] + r3b], axis=0), swap1)
    r2 = send(jnp.concatenate([g2[:lowf] + r3a, g2[lowf:]], axis=0), swap2)
    down_grad = (g0.astype(f32) + r1.astype(f32) + r2.astype(f32)).astype(bf16)[None]

    mine, other, tail = call(
        sum_kernel,
        [shape((rows_dev, part), bf16)] * 2 + [shape((rows_dev, 128), f32)],
        [VMEM] * 4,
        [],
        4 * rows_chip * part,
        12 * rows_chip * part,
    )(b0, from_above, from_below, from_far)
    if held > 1:
        mine, other, tail = [
            lax.all_to_all(
                array.reshape(held, capacity, array.shape[1]),
                "expert",
                0,
                0,
                axis_index_groups=across,
                tiled=True,
            ).reshape(array.shape)
            for array in (mine, other, tail)
        ]
    theirs = lax.ppermute(other, "dp", sibling)
    token_grad, logit_grad = call(
        lambda *refs: final_kernel(held, *refs),
        [
            shape((tok_count, width), bf16),
            shape((experts, tok_count), f32),
        ],
        [VMEM] * 7,
        [],
        2 * tok_count * rows_dev * width,
        2 * width * (tok_count + rows_dev),
    )(pick, mine, theirs, tail, chosen, inv_w, inv_total)
    return (token_grad, logit_grad.T, down_grad)


def solution(mesh):
    in_specs = (
        P(("expert", "dp"), None),
        P(("expert", "dp"), None),
        P(("expert", "dp"), None),
        P(("expert", "dp"), None),
        P("expert", None, None),
        P("expert", None, None),
        P("expert", None, None),
    )
    out_specs = (P(("expert", "dp"), None), P(("expert", "dp"), None), P("expert", None, "dp"))
    return jax.shard_map(
        per_device, mesh=mesh, in_specs=in_specs, out_specs=out_specs, check_vma=False
    )
```

```python
import jax
import jax.numpy as jnp
from jax import lax
from jax.experimental import pallas as pl
from jax.experimental.pallas import tpu as pltpu
from jax.sharding import PartitionSpec as P

SPLIT = 16
SCALE = 2.5
QUAD = 4
bf16 = jnp.bfloat16
f32 = jnp.float32
CONTRACT0 = (((0,), (0,)), ((), ()))
CONTRACT1 = (((1,), (1,)), ((), ()))
VMEM = pl.BlockSpec(memory_space=pltpu.VMEM)


def chunk_of(size, limit):
    best = 128
    for step in range(128, limit + 1, 128):
        if size % step == 0:
            best = step
    return best


def inner_chip():
    member = lax.rem(lax.axis_index("expert"), SPLIT) // QUAD
    return (member > 0) & (member < SPLIT // QUAD - 1)


def slot_rows(blocks, first, count, columns):
    own, far, ends, outer, middle = [b[first : first + count, columns] for b in blocks]
    return jnp.concatenate([own, far, ends, jnp.where(inner_chip(), middle, outer)], axis=0)


def split_of(total):
    return total // 2 // 256 * 256


def prep_kernel(held, capacity, *refs):
    gate, up, down, tokens, cotangent, logits, ids = refs[:7]
    weights, top, low, mine, other, pick_out = refs[7:13]
    chosen_out, inv_w_out, inv_total_out, sems = refs[13:]
    ff = gate.shape[2]
    part = mine.shape[2]
    wide = 2 * ff
    core = lax.axis_index("dp")
    start = pl.multiple_of(core * part, 128)
    away = pl.multiple_of((1 - core) * part, 128)
    split = top.shape[0]
    rest = part - split
    pairs = []
    for out, at, first, size in (
        (weights, 0, 0, part),
        (top, 0, 0, split),
        (low, 0, split, rest),
    ):
        rows = pl.ds(pl.multiple_of(start + first, 128), size)
        pairs.append((gate.at[0, rows, :], out.at[at : at + size, :ff]))
        pairs.append((up.at[0, rows, :], out.at[at : at + size, ff:]))
    for c in range(part // wide):
        columns = pl.ds(pl.multiple_of(start + c * wide, 128), wide)
        for out, at in ((weights, part), (low, rest)):
            rows = slice(at + c * ff, at + (c + 1) * ff)
            pairs.append((down.at[0, :, columns], out.at[rows, :]))
    copies = [
        pltpu.make_async_copy(src, dst, sems.at[i]) for i, (src, dst) in enumerate(pairs)
    ]
    for copy in copies:
        copy.start()

    experts, count = logits.shape
    expert = lax.broadcasted_iota(jnp.int32, (experts, count), 0)
    has = expert == ids[0:1, :]
    for k in range(1, ids.shape[0]):
        has = has | (expert == ids[k : k + 1, :])
    chosen = jnp.where(has, jax.nn.sigmoid(logits[...]), 0.0)
    total = jnp.sum(chosen, axis=0, keepdims=True)
    weight = (SCALE * chosen / total).astype(bf16).astype(f32)
    before = lax.broadcasted_iota(jnp.int32, (count, count), 0)
    after = lax.broadcasted_iota(jnp.int32, (count, count), 1)
    earlier = jnp.where(before < after, 1.0, 0.0).astype(bf16)
    named = jnp.where(has, 1.0, 0.0)
    rank = jnp.dot(named.astype(bf16), earlier, preferred_element_type=f32)
    slots = held * capacity
    slot = lax.broadcasted_iota(jnp.int32, (slots, count), 0)
    pick = jnp.zeros((slots, count), f32)
    value = jnp.zeros((slots, count), f32)
    for e in range(held):
        place = rank[e : e + 1, :].astype(jnp.int32) + e * capacity
        hit = jnp.where(slot == place, named[e : e + 1, :], 0.0)
        pick = pick + hit
        value = value + hit * weight[e : e + 1, :]
    value = jnp.sum(value, axis=1, keepdims=True)
    pick = pick.astype(bf16)
    pick_out[...] = pick
    chosen_out[...] = chosen
    inv_w_out[...] = jnp.where(has & (expert < held), 1.0 / weight, 0.0)
    inv_total_out[...] = jnp.broadcast_to(1.0 / total, chosen.shape)

    step = chunk_of(part, 512)

    def body(k, carry):
        at = pl.multiple_of(k * step, 128)
        for base, out in ((start, mine), (away, other)):
            columns = pl.ds(pl.multiple_of(base + at, 128), step)
            x = jnp.dot(pick, tokens[:, columns], preferred_element_type=f32)
            c = jnp.dot(pick, cotangent[:, columns], preferred_element_type=f32)
            out[0, :, pl.ds(at, step)] = x.astype(bf16)
            out[1, :, pl.ds(at, step)] = (c * value).astype(bf16)
        return carry

    lax.fori_loop(0, part // step, body, 0)
    for copy in copies:
        copy.wait()


def sum_kernel(own, far, ends, outer, middle, mine, other, tail):
    first = lax.axis_index("dp") == 0
    inner = inner_chip()
    rows, part = mine.shape
    step = chunk_of(part, 512)

    def total(columns):
        near = jnp.where(inner, 0.0, ends[:, columns].astype(f32))
        value = own[:, columns].astype(f32) + far[:, columns].astype(f32) + near
        value = value + outer[:, columns].astype(f32) + middle[:, columns].astype(f32)
        top, low = value[:rows], value[rows:]
        return jnp.where(first, top, low), jnp.where(first, low, top)

    def body(k, carry):
        columns = pl.ds(pl.multiple_of(k * step, 128), step)
        here, there = total(columns)
        mine[:, columns] = here.astype(bf16)
        other[:, columns] = there.astype(bf16)
        return carry

    lax.fori_loop(0, part // step, body, 0)
    tail[...] = total(slice(part, part + 128))[0]


def piece_sides(pieces):
    split = pieces[2].shape[0]
    upper = [(pieces[0], 0), (pieces[1], 0), (pieces[2], 0), (pieces[4], 0)]
    lower = [(pieces[0], split), (pieces[1], split), (pieces[3], 0), (pieces[5], 0)]
    return split, upper, lower


def gate_up_kernel(*refs):
    blocks, pieces, out = refs[:5], refs[5:-1], refs[-1]
    wide = pieces[0].shape[1]
    part = blocks[0].shape[1]
    count = out.shape[0] // (SPLIT // QUAD)
    split, upper, lower = piece_sides(pieces)
    out[...] = jnp.zeros_like(out)
    for side, first, size in ((upper, 0, split), (lower, split, part - split)):
        step = chunk_of(size, 1024)

        def body(k, carry):
            columns = pl.ds(pl.multiple_of(first + k * step, 128), step)
            x = slot_rows(blocks, 0, count, columns)
            for q, (ref, base) in enumerate(side):
                w = ref[pl.ds(pl.multiple_of(base + k * step, 128), step), :]
                out[:, q * wide : (q + 1) * wide] += jnp.dot(x, w, preferred_element_type=f32)
            return carry

        lax.fori_loop(0, size // step, body, 0)


def proj_kernel(*refs):
    blocks, pieces, out = refs[:5], refs[5:-1], refs[-1]
    wide = pieces[0].shape[1]
    ff = wide // 2
    part = blocks[0].shape[1]
    count = out.shape[0] // (SPLIT // QUAD)
    split, upper, lower = piece_sides(pieces)
    out[...] = jnp.zeros_like(out)

    def body(k, carry):
        columns = pl.ds(pl.multiple_of(k * wide, 128), wide)
        rows = slot_rows(blocks, count, count, columns)
        w = jnp.concatenate(
            [
                ref[pl.ds(pl.multiple_of(base + part - split + k * ff, 128), ff), :]
                for ref, base in lower
            ],
            axis=0,
        )
        out[...] += lax.dot_general(rows, w, CONTRACT1, preferred_element_type=f32)
        return carry

    lax.fori_loop(0, part // wide, body, 0)


def activations(mine, theirs, q, ff):
    base = 2 * q * ff
    g = mine[:, base : base + ff] + theirs[:, base : base + ff]
    u = mine[:, base + ff : base + 2 * ff] + theirs[:, base + ff : base + 2 * ff]
    sig = jax.nn.sigmoid(g)
    return g, u, sig, g * sig


def down_kernel(mine, theirs, *refs):
    blocks, outs, scratch = refs[:5], refs[5:-1], refs[-1]
    own, sent1, sent2, kept1, kept2 = outs
    ff, part = own.shape
    half = ff // 2
    count = scratch.shape[1] // (SPLIT // QUAD)
    step = chunk_of(part, 512)
    for q in range(QUAD):
        g, u, sig, active = activations(mine, theirs, q, ff)
        hidden = (active * u).astype(bf16).astype(f32)
        scratch[q * ff : (q + 1) * ff, :] = hidden.T.astype(bf16)

    def body(k, carry):
        columns = pl.ds(pl.multiple_of(k * step, 128), step)
        rows = slot_rows(blocks, count, count, columns)
        grads = jnp.dot(scratch[...], rows, preferred_element_type=f32).astype(bf16)
        g0, g1, g2, g3 = [grads[q * ff : (q + 1) * ff] for q in range(QUAD)]
        own[:, columns] = g0
        sent1[:, columns] = jnp.concatenate([g3[:half], g1[:half]], axis=0)
        sent2[:, columns] = jnp.concatenate([g3[half:], g2[half:]], axis=0)
        kept1[:, columns] = g1[half:]
        kept2[:, columns] = g2[:half]
        return carry

    lax.fori_loop(0, part // step, body, 0)


def back_kernel(mine, theirs, proj_mine, proj_theirs, *refs):
    members = SPLIT // QUAD
    pieces, outs, scratch = refs[: -members - 1], refs[-members - 1 : -1], refs[-1]
    wide = pieces[0].shape[1]
    ff = wide // 2
    rows = outs[0].shape[0]
    part = outs[0].shape[1] - 128
    split, upper, lower = piece_sides(pieces)
    dots = 0.0
    for q in range(QUAD):
        g, u, sig, active = activations(mine, theirs, q, ff)
        proj = proj_mine[:, q * ff : (q + 1) * ff] + proj_theirs[:, q * ff : (q + 1) * ff]
        hidden = (active * u).astype(bf16).astype(f32)
        dots = dots + jnp.sum(hidden * proj, axis=1, keepdims=True)
        base = 2 * q * ff
        scratch[:, base : base + ff] = (proj * u * sig * (1.0 + g * (1.0 - sig))).astype(bf16)
        scratch[:, base + ff : base + 2 * ff] = (proj * active).astype(bf16)

    high = dots.astype(bf16).astype(f32)
    rest = dots - high
    lane = lax.broadcasted_iota(jnp.int32, (rows, 128), 1)
    for i, out in enumerate(outs):
        at = 2 if i == 2 else 0
        top, low = high[i * rows : (i + 1) * rows], rest[i * rows : (i + 1) * rows]
        out[:, part : part + 128] = jnp.where(
            lane == at, top, jnp.where(lane == at + 1, low, 0.0)
        ).astype(bf16)
    for side, first, size in ((upper, 0, split), (lower, split, part - split)):
        step = chunk_of(size, 256)

        def body(k, carry):
            columns = pl.ds(pl.multiple_of(first + k * step, 128), step)
            w = jnp.concatenate(
                [ref[pl.ds(pl.multiple_of(base + k * step, 128), step), :] for ref, base in side],
                axis=1,
            )
            grads = lax.dot_general(scratch[...], w, CONTRACT1, preferred_element_type=f32)
            for i, out in enumerate(outs):
                out[:, columns] = grads[i * rows : (i + 1) * rows].astype(bf16)
            return carry

        lax.fori_loop(0, size // step, body, 0)


def final_kernel(held, pick, mine, theirs, tail, chosen, inv_w, inv_total, tok_out, logit_out):
    core = lax.axis_index("dp")
    slots, part = mine.shape
    step = chunk_of(part, 512)
    pick_t = pick[...]

    def body(k, carry):
        at = pl.multiple_of(k * step, 128)
        for source, side in ((mine, core), (theirs, 1 - core)):
            block = lax.dot_general(
                pick_t, source[:, pl.ds(at, step)], CONTRACT0, preferred_element_type=f32
            )
            tok_out[:, pl.ds(pl.multiple_of(side * part + at, 128), step)] = block.astype(bf16)
        return carry

    lax.fori_loop(0, part // step, body, 0)
    values = jnp.sum(tail[...], axis=1, keepdims=True)
    entries = pick_t.astype(f32) * values
    full = chosen.shape
    expert = lax.broadcasted_iota(jnp.int32, full, 0)
    slot = lax.broadcasted_iota(jnp.int32, entries.shape, 0)
    capacity = slots // held
    dw = jnp.zeros(full, f32)
    for e in range(held):
        inside = (slot >= e * capacity) & (slot < (e + 1) * capacity)
        found = jnp.sum(jnp.where(inside, entries, 0.0), axis=0, keepdims=True)
        dw = jnp.where(expert == e, jnp.broadcast_to(found, full), dw)
    dw = dw * inv_w[...]
    share = chosen[...]
    inner = jnp.sum(dw * share, axis=0, keepdims=True) * inv_total[...]
    logit_out[...] = SCALE * inv_total[...] * (dw - inner) * share * (1.0 - share)


def call(kernel, outs, in_specs, scratch, flops, moved, limit=40, out_specs=None):
    return pl.pallas_call(
        kernel,
        out_shape=outs,
        in_specs=in_specs,
        out_specs=out_specs or [VMEM] * len(outs),
        scratch_shapes=scratch,
        compiler_params=pltpu.CompilerParams(vmem_limit_bytes=limit * 1024 * 1024),
        cost_estimate=pl.CostEstimate(flops=flops, bytes_accessed=moved, transcendentals=0),
    )


def per_device(tokens, cotangent, logits, expert_ids, gate_proj, up_proj, down_proj):
    devices = lax.axis_size("expert")
    cores = lax.axis_size("dp")
    core = lax.axis_index("dp")
    held = devices // SPLIT
    tok_count, top = expert_ids.shape
    experts = logits.shape[1]
    width = tokens.shape[1]
    ff = gate_proj.shape[2]
    part = width // cores
    capacity = max(2, 5 * tok_count * top // (4 * experts))
    members = SPLIT // QUAD
    rows_dev = held * capacity
    rows_chip = cores * rows_dev
    slots = members * rows_chip
    across = [[e * SPLIT + j for e in range(held)] for j in range(SPLIT)]
    swap1 = [(i, i ^ 1) for i in range(devices)]
    swap2 = [(i, i ^ 2) for i in range(devices)]
    sibling = [(c, cores - 1 - c) for c in range(cores)]
    barrier = lax.optimization_barrier

    def send(array, route):
        return lax.ppermute(array, "expert", route)

    def line(pairs):
        return [
            (e * SPLIT + a * QUAD + q, e * SPLIT + b * QUAD + q)
            for e in range(held)
            for a, b in pairs
            for q in range(QUAD)
        ]

    distant = line([(m, m ^ 2) for m in range(members)])
    outward = line([(1, 0), (2, 3)])
    inward = line([(0, 1), (3, 2)])
    middle_swap = line([(1, 2), (2, 1)])
    inner = inner_chip()

    lowf = ff // 2
    packed = part + part // 2
    split = split_of(packed)
    shape = jax.ShapeDtypeStruct
    hbm = pl.BlockSpec(memory_space=pltpu.HBM)
    weights, w_top, w_low, mine, other, pick, chosen, inv_w, inv_total = call(
        lambda *refs: prep_kernel(held, capacity, *refs),
        [shape((size, 2 * ff), bf16) for size in (packed, split, packed - split)]
        + [shape((2, rows_dev, part), bf16)] * 2
        + [shape((rows_dev, tok_count), bf16)]
        + [shape((experts, tok_count), f32)] * 3,
        [hbm] * 3 + [VMEM] * 4,
        [pltpu.SemaphoreType.DMA((6 + part // ff,))],
        4 * rows_dev * tok_count * width,
        12 * part * ff + 4 * tok_count * width,
        limit=58,
        out_specs=[hbm] * 3 + [VMEM] * 6,
    )(gate_proj, up_proj, down_proj, tokens, cotangent, logits.T, expert_ids.T)
    w1 = send(weights, swap1)
    w2_top = send(w_top, swap2)
    w2_low = send(w_low, swap2)

    theirs = lax.ppermute(other, "dp", sibling)
    own = jnp.concatenate(
        [
            jnp.where(core == (0 if side == 0 else cores - 1), mine[i], theirs[i])
            for i in range(2)
            for side in range(cores)
        ],
        axis=0,
    )
    if held > 1:
        own = own.reshape(2, cores, held, capacity, part)
        own = lax.all_to_all(own, "expert", 2, 2, axis_index_groups=across, tiled=True)
        own = own.reshape(2 * rows_chip, part)
    far = send(own, distant)
    outer = send(own, outward)
    w1, w2_top, w2_low, own, far, outer = barrier((w1, w2_top, w2_low, own, far, outer))
    w3_top = send(w2_top, swap1)
    w3_low = send(w1[split:], swap2)
    ends = send(jnp.where(inner, far, own), outward + inward)
    middle = send(own, middle_swap)
    w = [weights, w1, w2_top, w2_low, w3_top, w3_low]
    blocks = [own, far, ends, outer, middle]

    matmul = 2 * slots * part * QUAD * ff
    (g_u,) = call(
        gate_up_kernel,
        [shape((slots, QUAD * 2 * ff), f32)],
        [VMEM] * 11,
        [],
        2 * matmul,
        2 * part * (slots + QUAD * 2 * ff),
    )(*blocks, *w)
    g_u_sib = lax.ppermute(g_u, "dp", sibling)
    (proj,) = call(
        proj_kernel,
        [shape((slots, QUAD * ff), f32)],
        [VMEM] * 11,
        [],
        matmul,
        2 * part * (slots + QUAD * ff),
    )(*blocks, *w)
    proj_sib = lax.ppermute(proj, "dp", sibling)
    g0, sent1, sent2, kept1, kept2 = call(
        down_kernel,
        [shape((ff, part), bf16)] * 3 + [shape((lowf, part), bf16)] * 2,
        [VMEM] * 7,
        [pltpu.VMEM((QUAD * ff, slots), bf16)],
        matmul,
        2 * part * (slots + QUAD * ff),
    )(g_u, g_u_sib, *blocks)
    g0, sent1, sent2, proj, proj_sib = barrier((g0, sent1, sent2, proj, proj_sib))
    got1 = send(sent1, swap1)
    got2 = send(sent2, swap2)
    b0, b1, b2, b3 = call(
        back_kernel,
        [shape((rows_chip, part + 128), bf16)] * members,
        [VMEM] * 10,
        [pltpu.VMEM((slots, QUAD * 2 * ff), bf16)],
        2 * matmul,
        2 * part * (slots + QUAD * 2 * ff),
    )(g_u, g_u_sib, proj, proj_sib, *w)

    ends = send(b2, outward + inward)
    middle = send(b3, middle_swap)
    ends, middle, got1, got2, b1, b3 = barrier((ends, middle, got1, got2, b1, b3))
    joined = b1 + jnp.where(inner, ends, jnp.zeros((), bf16))
    joined, got1, got2 = barrier((joined, got1, got2))
    far = send(joined, distant)
    outer = send(b3, inward)
    got3 = send(kept1 + got2[:lowf], swap1)
    got4 = send(kept2 + got1[:lowf], swap2)
    mine, other, tail = call(
        sum_kernel,
        [shape((rows_dev, part), bf16)] * 2 + [shape((rows_dev, 128), f32)],
        [VMEM] * 5,
        [],
        matmul,
        12 * rows_chip * part,
    )(b0, far, ends, outer, middle)
    other, got3, got4 = barrier((other, got3, got4))
    add = lambda a, b, c: (a.astype(f32) + b.astype(f32) + c.astype(f32)).astype(bf16)
    down_grad = jnp.concatenate(
        [add(g0[:lowf], got1[lowf:], got4), add(g0[lowf:], got2[lowf:], got3)], axis=0
    )[None]
    if held > 1:
        mine, other, tail = [
            lax.all_to_all(
                array.reshape(held, capacity, array.shape[1]),
                "expert",
                0,
                0,
                axis_index_groups=across,
                tiled=True,
            ).reshape(array.shape)
            for array in (mine, other, tail)
        ]
    theirs = lax.ppermute(other, "dp", sibling)
    token_grad, logit_grad = call(
        lambda *refs: final_kernel(held, *refs),
        [
            shape((tok_count, width), bf16),
            shape((experts, tok_count), f32),
        ],
        [VMEM] * 7,
        [],
        2 * tok_count * rows_dev * width,
        2 * width * (tok_count + rows_dev),
    )(pick, mine, theirs, tail, chosen, inv_w, inv_total)
    return (token_grad, logit_grad.T, down_grad)


def solution(mesh):
    in_specs = (
        P(("expert", "dp"), None),
        P(("expert", "dp"), None),
        P(("expert", "dp"), None),
        P(("expert", "dp"), None),
        P("expert", None, None),
        P("expert", None, None),
        P("expert", None, None),
    )
    out_specs = (P(("expert", "dp"), None), P(("expert", "dp"), None), P("expert", None, "dp"))
    return jax.shard_map(
        per_device, mesh=mesh, in_specs=in_specs, out_specs=out_specs, check_vma=False
    )
```

```python
import jax
import jax.numpy as jnp
from jax import lax
from jax.experimental import pallas as pl
from jax.experimental.pallas import tpu as pltpu
from jax.sharding import PartitionSpec as P

SPLIT = 16
SCALE = 2.5
QUAD = 4
bf16 = jnp.bfloat16
f32 = jnp.float32
CONTRACT0 = (((0,), (0,)), ((), ()))
CONTRACT1 = (((1,), (1,)), ((), ()))
VMEM = pl.BlockSpec(memory_space=pltpu.VMEM)


def chunk_of(size, limit):
    best = 128
    for step in range(128, limit + 1, 128):
        if size % step == 0:
            best = step
    return best


def inner_chip():
    member = lax.rem(lax.axis_index("expert"), SPLIT) // QUAD
    return (member > 0) & (member < SPLIT // QUAD - 1)


def slot_rows(blocks, first, count, columns):
    own, far, ends, outer, middle = [b[first : first + count, columns] for b in blocks]
    return jnp.concatenate([own, far, ends, jnp.where(inner_chip(), middle, outer)], axis=0)


def split_of(total):
    return total // 2 // 256 * 256


def prep_kernel(held, capacity, *refs):
    gate, up, down, tokens, cotangent, logits, ids = refs[:7]
    weights, top, low, mine, other, pick_out = refs[7:13]
    chosen_out, inv_w_out, inv_total_out, packed, sems = refs[13:]
    ff = gate.shape[2]
    part = mine.shape[2]
    wide = 2 * ff
    core = lax.axis_index("dp")
    start = pl.multiple_of(core * part, 128)
    away = pl.multiple_of((1 - core) * part, 128)
    split = top.shape[0]
    half = pl.ds(start, part)
    pairs = [
        (gate.at[0, half, :], packed.at[:part, :ff]),
        (up.at[0, half, :], packed.at[:part, ff:]),
    ]
    for c in range(part // wide):
        columns = pl.ds(pl.multiple_of(start + c * wide, 128), wide)
        pairs.append((down.at[0, :, columns], packed.at[part + c * ff : part + (c + 1) * ff, :]))
    reads = len(pairs)
    pairs += [(packed, weights), (packed.at[:split, :], top), (packed.at[split:, :], low)]
    copies = [
        pltpu.make_async_copy(src, dst, sems.at[i]) for i, (src, dst) in enumerate(pairs)
    ]
    for copy in copies[:reads]:
        copy.start()

    experts, count = logits.shape
    expert = lax.broadcasted_iota(jnp.int32, (experts, count), 0)
    has = expert == ids[0:1, :]
    for k in range(1, ids.shape[0]):
        has = has | (expert == ids[k : k + 1, :])
    chosen = jnp.where(has, jax.nn.sigmoid(logits[...]), 0.0)
    total = jnp.sum(chosen, axis=0, keepdims=True)
    weight = (SCALE * chosen / total).astype(bf16).astype(f32)
    before = lax.broadcasted_iota(jnp.int32, (count, count), 0)
    after = lax.broadcasted_iota(jnp.int32, (count, count), 1)
    earlier = jnp.where(before < after, 1.0, 0.0).astype(bf16)
    named = jnp.where(has, 1.0, 0.0)
    rank = jnp.dot(named.astype(bf16), earlier, preferred_element_type=f32)
    slots = held * capacity
    slot = lax.broadcasted_iota(jnp.int32, (slots, count), 0)
    pick = jnp.zeros((slots, count), f32)
    value = jnp.zeros((slots, count), f32)
    for e in range(held):
        place = rank[e : e + 1, :].astype(jnp.int32) + e * capacity
        hit = jnp.where(slot == place, named[e : e + 1, :], 0.0)
        pick = pick + hit
        value = value + hit * weight[e : e + 1, :]
    value = jnp.sum(value, axis=1, keepdims=True)
    pick = pick.astype(bf16)
    pick_out[...] = pick
    chosen_out[...] = chosen
    inv_w_out[...] = jnp.where(has & (expert < held), 1.0 / weight, 0.0)
    inv_total_out[...] = jnp.broadcast_to(1.0 / total, chosen.shape)

    step = chunk_of(part, 512)

    def body(k, carry):
        at = pl.multiple_of(k * step, 128)
        for base, out in ((start, mine), (away, other)):
            columns = pl.ds(pl.multiple_of(base + at, 128), step)
            x = jnp.dot(pick, tokens[:, columns], preferred_element_type=f32)
            c = jnp.dot(pick, cotangent[:, columns], preferred_element_type=f32)
            out[0, :, pl.ds(at, step)] = x.astype(bf16)
            out[1, :, pl.ds(at, step)] = (c * value).astype(bf16)
        return carry

    for copy in copies[:reads]:
        copy.wait()
    for copy in copies[reads:]:
        copy.start()
    lax.fori_loop(0, part // step, body, 0)
    for copy in copies[reads:]:
        copy.wait()


def sum_kernel(own, far, ends, outer, middle, mine, other, tail):
    first = lax.axis_index("dp") == 0
    inner = inner_chip()
    rows, part = mine.shape
    step = chunk_of(part, 512)

    def total(columns):
        near = jnp.where(inner, 0.0, ends[:, columns].astype(f32))
        value = own[:, columns].astype(f32) + far[:, columns].astype(f32) + near
        value = value + outer[:, columns].astype(f32) + middle[:, columns].astype(f32)
        top, low = value[:rows], value[rows:]
        return jnp.where(first, top, low), jnp.where(first, low, top)

    def body(k, carry):
        columns = pl.ds(pl.multiple_of(k * step, 128), step)
        here, there = total(columns)
        mine[:, columns] = here.astype(bf16)
        other[:, columns] = there.astype(bf16)
        return carry

    lax.fori_loop(0, part // step, body, 0)
    tail[...] = total(slice(part, part + 128))[0]


def piece_sides(pieces):
    split = pieces[2].shape[0]
    upper = [(pieces[0], 0), (pieces[1], 0), (pieces[2], 0), (pieces[4], 0)]
    lower = [(pieces[0], split), (pieces[1], split), (pieces[3], 0), (pieces[5], 0)]
    return split, upper, lower


def gate_up_kernel(*refs):
    blocks, pieces, out = refs[:5], refs[5:-1], refs[-1]
    wide = pieces[0].shape[1]
    part = blocks[0].shape[1]
    count = out.shape[0] // (SPLIT // QUAD)
    split, upper, lower = piece_sides(pieces)
    out[...] = jnp.zeros_like(out)
    for side, first, size in ((upper, 0, split), (lower, split, part - split)):
        step = chunk_of(size, 1024)

        def body(k, carry):
            columns = pl.ds(pl.multiple_of(first + k * step, 128), step)
            x = slot_rows(blocks, 0, count, columns)
            for q, (ref, base) in enumerate(side):
                w = ref[pl.ds(pl.multiple_of(base + k * step, 128), step), :]
                out[:, q * wide : (q + 1) * wide] += jnp.dot(x, w, preferred_element_type=f32)
            return carry

        lax.fori_loop(0, size // step, body, 0)


def proj_kernel(*refs):
    blocks, pieces, out = refs[:5], refs[5:-1], refs[-1]
    wide = pieces[0].shape[1]
    ff = wide // 2
    part = blocks[0].shape[1]
    count = out.shape[0] // (SPLIT // QUAD)
    split, upper, lower = piece_sides(pieces)
    out[...] = jnp.zeros_like(out)

    pair = 2 if part // wide % 2 == 0 else 1
    step = pair * wide

    def body(k, carry):
        columns = pl.ds(pl.multiple_of(k * step, 128), step)
        rows = slot_rows(blocks, count, count, columns)
        w = jnp.concatenate(
            [
                jnp.concatenate(
                    [
                        ref[pl.ds(pl.multiple_of(base + part - split + (pair * k + i) * ff, 128), ff), :]
                        for i in range(pair)
                    ],
                    axis=1,
                )
                for ref, base in lower
            ],
            axis=0,
        )
        out[...] += lax.dot_general(rows, w, CONTRACT1, preferred_element_type=f32)
        return carry

    lax.fori_loop(0, part // step, body, 0)


def activations(mine, theirs, q, ff):
    base = 2 * q * ff
    g = mine[:, base : base + ff] + theirs[:, base : base + ff]
    u = mine[:, base + ff : base + 2 * ff] + theirs[:, base + ff : base + 2 * ff]
    sig = jax.nn.sigmoid(g)
    return g, u, sig, g * sig


def down_kernel(mine, theirs, *refs):
    blocks, outs, scratch = refs[:5], refs[5:-1], refs[-1]
    own, sent1, sent2, kept1, kept2 = outs
    ff, part = own.shape
    half = ff // 2
    count = scratch.shape[1] // (SPLIT // QUAD)
    step = chunk_of(part, 512)
    for q in range(QUAD):
        g, u, sig, active = activations(mine, theirs, q, ff)
        hidden = (active * u).astype(bf16).astype(f32)
        scratch[q * ff : (q + 1) * ff, :] = hidden.T.astype(bf16)

    def body(k, carry):
        columns = pl.ds(pl.multiple_of(k * step, 128), step)
        rows = slot_rows(blocks, count, count, columns)
        grads = jnp.dot(scratch[...], rows, preferred_element_type=f32).astype(bf16)
        g0, g1, g2, g3 = [grads[q * ff : (q + 1) * ff] for q in range(QUAD)]
        own[:, columns] = g0
        sent1[:, columns] = jnp.concatenate([g3[:half], g1[:half]], axis=0)
        sent2[:, columns] = jnp.concatenate([g3[half:], g2[half:]], axis=0)
        kept1[:, columns] = g1[half:]
        kept2[:, columns] = g2[:half]
        return carry

    lax.fori_loop(0, part // step, body, 0)


def back_kernel(mine, theirs, proj_mine, proj_theirs, *refs):
    members = SPLIT // QUAD
    pieces, outs, scratch = refs[: -members - 1], refs[-members - 1 : -1], refs[-1]
    wide = pieces[0].shape[1]
    ff = wide // 2
    rows = outs[0].shape[0]
    part = outs[0].shape[1] - 128
    split, upper, lower = piece_sides(pieces)
    dots = 0.0
    for q in range(QUAD):
        g, u, sig, active = activations(mine, theirs, q, ff)
        proj = proj_mine[:, q * ff : (q + 1) * ff] + proj_theirs[:, q * ff : (q + 1) * ff]
        hidden = (active * u).astype(bf16).astype(f32)
        dots = dots + jnp.sum(hidden * proj, axis=1, keepdims=True)
        base = 2 * q * ff
        scratch[:, base : base + ff] = (proj * u * sig * (1.0 + g * (1.0 - sig))).astype(bf16)
        scratch[:, base + ff : base + 2 * ff] = (proj * active).astype(bf16)

    high = dots.astype(bf16).astype(f32)
    rest = dots - high
    lane = lax.broadcasted_iota(jnp.int32, (rows, 128), 1)
    for i, out in enumerate(outs):
        at = 2 if i == 2 else 0
        top, low = high[i * rows : (i + 1) * rows], rest[i * rows : (i + 1) * rows]
        out[:, part : part + 128] = jnp.where(
            lane == at, top, jnp.where(lane == at + 1, low, 0.0)
        ).astype(bf16)
    for side, first, size in ((upper, 0, split), (lower, split, part - split)):
        step = chunk_of(size, 256)

        def body(k, carry):
            columns = pl.ds(pl.multiple_of(first + k * step, 128), step)
            w = jnp.concatenate(
                [ref[pl.ds(pl.multiple_of(base + k * step, 128), step), :] for ref, base in side],
                axis=1,
            )
            grads = lax.dot_general(scratch[...], w, CONTRACT1, preferred_element_type=f32)
            for i, out in enumerate(outs):
                out[:, columns] = grads[i * rows : (i + 1) * rows].astype(bf16)
            return carry

        lax.fori_loop(0, size // step, body, 0)


def final_kernel(held, pick, mine, theirs, tail, chosen, inv_w, inv_total, tok_out, logit_out):
    core = lax.axis_index("dp")
    slots, part = mine.shape
    step = chunk_of(part, 512)
    pick_t = pick[...]

    def body(k, carry):
        at = pl.multiple_of(k * step, 128)
        for source, side in ((mine, core), (theirs, 1 - core)):
            block = lax.dot_general(
                pick_t, source[:, pl.ds(at, step)], CONTRACT0, preferred_element_type=f32
            )
            tok_out[:, pl.ds(pl.multiple_of(side * part + at, 128), step)] = block.astype(bf16)
        return carry

    lax.fori_loop(0, part // step, body, 0)
    values = jnp.sum(tail[...], axis=1, keepdims=True)
    entries = pick_t.astype(f32) * values
    full = chosen.shape
    expert = lax.broadcasted_iota(jnp.int32, full, 0)
    slot = lax.broadcasted_iota(jnp.int32, entries.shape, 0)
    capacity = slots // held
    dw = jnp.zeros(full, f32)
    for e in range(held):
        inside = (slot >= e * capacity) & (slot < (e + 1) * capacity)
        found = jnp.sum(jnp.where(inside, entries, 0.0), axis=0, keepdims=True)
        dw = jnp.where(expert == e, jnp.broadcast_to(found, full), dw)
    dw = dw * inv_w[...]
    share = chosen[...]
    inner = jnp.sum(dw * share, axis=0, keepdims=True) * inv_total[...]
    logit_out[...] = SCALE * inv_total[...] * (dw - inner) * share * (1.0 - share)


def call(kernel, outs, in_specs, scratch, flops, moved, limit=20, out_specs=None):
    return pl.pallas_call(
        kernel,
        out_shape=outs,
        in_specs=in_specs,
        out_specs=out_specs or [VMEM] * len(outs),
        scratch_shapes=scratch,
        compiler_params=pltpu.CompilerParams(vmem_limit_bytes=limit * 1024 * 1024),
        cost_estimate=pl.CostEstimate(flops=flops, bytes_accessed=moved, transcendentals=0),
    )


def per_device(tokens, cotangent, logits, expert_ids, gate_proj, up_proj, down_proj):
    devices = lax.axis_size("expert")
    cores = lax.axis_size("dp")
    core = lax.axis_index("dp")
    held = devices // SPLIT
    tok_count, top = expert_ids.shape
    experts = logits.shape[1]
    width = tokens.shape[1]
    ff = gate_proj.shape[2]
    part = width // cores
    capacity = max(2, 5 * tok_count * top // (4 * experts))
    members = SPLIT // QUAD
    rows_dev = held * capacity
    rows_chip = cores * rows_dev
    slots = members * rows_chip
    across = [[e * SPLIT + j for e in range(held)] for j in range(SPLIT)]
    swap1 = [(i, i ^ 1) for i in range(devices)]
    swap2 = [(i, i ^ 2) for i in range(devices)]
    sibling = [(c, cores - 1 - c) for c in range(cores)]
    barrier = lax.optimization_barrier

    def send(array, route):
        return lax.ppermute(array, "expert", route)

    def line(pairs):
        return [
            (e * SPLIT + a * QUAD + q, e * SPLIT + b * QUAD + q)
            for e in range(held)
            for a, b in pairs
            for q in range(QUAD)
        ]

    distant = line([(m, m ^ 2) for m in range(members)])
    outward = line([(1, 0), (2, 3)])
    inward = line([(0, 1), (3, 2)])
    middle_swap = line([(1, 2), (2, 1)])
    inner = inner_chip()

    lowf = ff // 2
    packed = part + part // 2
    split = split_of(packed)
    shape = jax.ShapeDtypeStruct
    hbm = pl.BlockSpec(memory_space=pltpu.HBM)
    weights, w_top, w_low, mine, other, pick, chosen, inv_w, inv_total = call(
        lambda *refs: prep_kernel(held, capacity, *refs),
        [shape((size, 2 * ff), bf16) for size in (packed, split, packed - split)]
        + [shape((2, rows_dev, part), bf16)] * 2
        + [shape((rows_dev, tok_count), bf16)]
        + [shape((experts, tok_count), f32)] * 3,
        [hbm] * 3 + [VMEM] * 4,
        [pltpu.VMEM((packed, 2 * ff), bf16), pltpu.SemaphoreType.DMA((5 + part // (2 * ff),))],
        4 * rows_dev * tok_count * width,
        12 * part * ff + 4 * tok_count * width,
        limit=58,
        out_specs=[hbm] * 3 + [VMEM] * 6,
    )(gate_proj, up_proj, down_proj, tokens, cotangent, logits.T, expert_ids.T)
    w1 = send(weights, swap1)
    w2_top = send(w_top, swap2)
    w2_low = send(w_low, swap2)

    theirs = lax.ppermute(other, "dp", sibling)
    own = jnp.concatenate(
        [
            jnp.where(core == (0 if side == 0 else cores - 1), mine[i], theirs[i])
            for i in range(2)
            for side in range(cores)
        ],
        axis=0,
    )
    if held > 1:
        own = own.reshape(2, cores, held, capacity, part)
        own = lax.all_to_all(own, "expert", 2, 2, axis_index_groups=across, tiled=True)
        own = own.reshape(2 * rows_chip, part)
    far = send(own, distant)
    outer = send(own, outward)
    w1, w2_top, w2_low, own, far, outer = barrier((w1, w2_top, w2_low, own, far, outer))
    w3_top = send(w2_top, swap1)
    w3_low = send(w1[split:], swap2)
    ends = send(jnp.where(inner, far, own), outward + inward)
    middle = send(own, middle_swap)
    w = [weights, w1, w2_top, w2_low, w3_top, w3_low]
    blocks = [own, far, ends, outer, middle]

    matmul = 2 * slots * part * QUAD * ff
    (g_u,) = call(
        gate_up_kernel,
        [shape((slots, QUAD * 2 * ff), f32)],
        [VMEM] * 11,
        [],
        2 * matmul,
        2 * part * (slots + QUAD * 2 * ff),
    )(*blocks, *w)
    g_u_sib = lax.ppermute(g_u, "dp", sibling)
    (proj,) = call(
        proj_kernel,
        [shape((slots, QUAD * ff), f32)],
        [VMEM] * 11,
        [],
        matmul,
        2 * part * (slots + QUAD * ff),
    )(*blocks, *w)
    proj_sib = lax.ppermute(proj, "dp", sibling)
    g0, sent1, sent2, kept1, kept2 = call(
        down_kernel,
        [shape((ff, part), bf16)] * 3 + [shape((lowf, part), bf16)] * 2,
        [VMEM] * 7,
        [pltpu.VMEM((QUAD * ff, slots), bf16)],
        matmul,
        2 * part * (slots + QUAD * ff),
    )(g_u, g_u_sib, *blocks)
    g0, sent1, sent2, proj, proj_sib = barrier((g0, sent1, sent2, proj, proj_sib))
    got1 = send(sent1, swap1)
    got2 = send(sent2, swap2)
    b0, b1, b2, b3 = call(
        back_kernel,
        [shape((rows_chip, part + 128), bf16)] * members,
        [VMEM] * 10,
        [pltpu.VMEM((slots, QUAD * 2 * ff), bf16)],
        2 * matmul,
        2 * part * (slots + QUAD * 2 * ff),
    )(g_u, g_u_sib, proj, proj_sib, *w)

    ends = send(b2, outward + inward)
    middle = send(b3, middle_swap)
    ends, middle, got1, got2, b1, b3 = barrier((ends, middle, got1, got2, b1, b3))
    joined = b1 + jnp.where(inner, ends, jnp.zeros((), bf16))
    joined, got1, got2 = barrier((joined, got1, got2))
    far = send(joined, distant)
    outer = send(b3, inward)
    got3 = send(kept1 + got2[:lowf], swap1)
    got4 = send(kept2 + got1[:lowf], swap2)
    mine, other, tail = call(
        sum_kernel,
        [shape((rows_dev, part), bf16)] * 2 + [shape((rows_dev, 128), f32)],
        [VMEM] * 5,
        [],
        matmul,
        12 * rows_chip * part,
    )(b0, far, ends, outer, middle)
    other, got3, got4 = barrier((other, got3, got4))
    add = lambda a, b, c: (a.astype(f32) + b.astype(f32) + c.astype(f32)).astype(bf16)
    down_grad = jnp.concatenate(
        [add(g0[:lowf], got1[lowf:], got4), add(g0[lowf:], got2[lowf:], got3)], axis=0
    )[None]
    if held > 1:
        mine, other, tail = [
            lax.all_to_all(
                array.reshape(held, capacity, array.shape[1]),
                "expert",
                0,
                0,
                axis_index_groups=across,
                tiled=True,
            ).reshape(array.shape)
            for array in (mine, other, tail)
        ]
    theirs = lax.ppermute(other, "dp", sibling)
    token_grad, logit_grad = call(
        lambda *refs: final_kernel(held, *refs),
        [
            shape((tok_count, width), bf16),
            shape((experts, tok_count), f32),
        ],
        [VMEM] * 7,
        [],
        2 * tok_count * rows_dev * width,
        2 * width * (tok_count + rows_dev),
    )(pick, mine, theirs, tail, chosen, inv_w, inv_total)
    return (token_grad, logit_grad.T, down_grad)


def solution(mesh):
    in_specs = (
        P(("expert", "dp"), None),
        P(("expert", "dp"), None),
        P(("expert", "dp"), None),
        P(("expert", "dp"), None),
        P("expert", None, None),
        P("expert", None, None),
        P("expert", None, None),
    )
    out_specs = (P(("expert", "dp"), None), P(("expert", "dp"), None), P("expert", None, "dp"))
    return jax.shard_map(
        per_device, mesh=mesh, in_specs=in_specs, out_specs=out_specs, check_vma=False
    )
```

```python
import jax
import jax.numpy as jnp
from jax import lax
from jax.experimental import pallas as pl
from jax.experimental.pallas import tpu as pltpu
from jax.sharding import PartitionSpec as P

SPLIT = 16
SCALE = 2.5
QUAD = 4
bf16 = jnp.bfloat16
f32 = jnp.float32
CONTRACT0 = (((0,), (0,)), ((), ()))
CONTRACT1 = (((1,), (1,)), ((), ()))
VMEM = pl.BlockSpec(memory_space=pltpu.VMEM)


def chunk_of(size, limit):
    best = 128
    for step in range(128, limit + 1, 128):
        if size % step == 0:
            best = step
    return best


def inner_chip():
    member = lax.rem(lax.axis_index("expert"), SPLIT) // QUAD
    return (member > 0) & (member < SPLIT // QUAD - 1)


def slot_rows(blocks):
    own, far, ends, outer, middle = [b[...] for b in blocks]
    return jnp.concatenate([own, far, ends, jnp.where(inner_chip(), middle, outer)], axis=0)


def split_of(total):
    return total // 2 // 256 * 256


def pack_kernel(gate, up, down, weights, top, low, packed, sems):
    ff = gate.shape[2]
    wide = 2 * ff
    part = packed.shape[0] * 2 // 3
    split = top.shape[0]
    start = pl.multiple_of(lax.axis_index("dp") * part, 128)
    half = pl.ds(start, part)
    pairs = [
        (gate.at[0, half, :], packed.at[:part, :ff]),
        (up.at[0, half, :], packed.at[:part, ff:]),
    ]
    for c in range(part // wide):
        columns = pl.ds(pl.multiple_of(start + c * wide, 128), wide)
        pairs.append((down.at[0, :, columns], packed.at[part + c * ff : part + (c + 1) * ff, :]))
    reads = len(pairs)
    pairs += [(packed, weights), (packed.at[:split, :], top), (packed.at[split:, :], low)]
    copies = [
        pltpu.make_async_copy(src, dst, sems.at[i]) for i, (src, dst) in enumerate(pairs)
    ]
    for copy in copies[:reads]:
        copy.start()
    for copy in copies[:reads]:
        copy.wait()
    for copy in copies[reads:]:
        copy.start()
    for copy in copies[reads:]:
        copy.wait()


def arrived_kernel(w1, w2_top, w2_low, mark):
    mark[...] = jnp.zeros_like(mark)


def prep_kernel(held, capacity, *refs):
    tokens, cotangent, logits, ids = refs[:4]
    mine, other, pick_out, chosen_out, inv_w_out, inv_total_out = refs[4:]
    part = mine.shape[2]
    core = lax.axis_index("dp")
    start = pl.multiple_of(core * part, 128)
    away = pl.multiple_of((1 - core) * part, 128)

    experts, count = logits.shape
    expert = lax.broadcasted_iota(jnp.int32, (experts, count), 0)
    has = expert == ids[0:1, :]
    for k in range(1, ids.shape[0]):
        has = has | (expert == ids[k : k + 1, :])
    chosen = jnp.where(has, jax.nn.sigmoid(logits[...]), 0.0)
    total = jnp.sum(chosen, axis=0, keepdims=True)
    weight = (SCALE * chosen / total).astype(bf16).astype(f32)
    before = lax.broadcasted_iota(jnp.int32, (count, count), 0)
    after = lax.broadcasted_iota(jnp.int32, (count, count), 1)
    earlier = jnp.where(before < after, 1.0, 0.0).astype(bf16)
    named = jnp.where(has, 1.0, 0.0)
    rank = jnp.dot(named.astype(bf16), earlier, preferred_element_type=f32)
    slots = held * capacity
    slot = lax.broadcasted_iota(jnp.int32, (slots, count), 0)
    pick = jnp.zeros((slots, count), f32)
    value = jnp.zeros((slots, count), f32)
    for e in range(held):
        place = rank[e : e + 1, :].astype(jnp.int32) + e * capacity
        hit = jnp.where(slot == place, named[e : e + 1, :], 0.0)
        pick = pick + hit
        value = value + hit * weight[e : e + 1, :]
    value = jnp.sum(value, axis=1, keepdims=True)
    pick = pick.astype(bf16)
    pick_out[...] = pick
    chosen_out[...] = chosen
    inv_w_out[...] = jnp.where(has & (expert < held), 1.0 / weight, 0.0)
    inv_total_out[...] = jnp.broadcast_to(1.0 / total, chosen.shape)

    step = chunk_of(part, 512)

    def body(k, carry):
        at = pl.multiple_of(k * step, 128)
        for base, out in ((start, mine), (away, other)):
            columns = pl.ds(pl.multiple_of(base + at, 128), step)
            x = jnp.dot(pick, tokens[:, columns], preferred_element_type=f32)
            c = jnp.dot(pick, cotangent[:, columns], preferred_element_type=f32)
            out[0, :, pl.ds(at, step)] = x.astype(bf16)
            out[1, :, pl.ds(at, step)] = (c * value).astype(bf16)
        return carry

    lax.fori_loop(0, part // step, body, 0)


def sum_kernel(own, far, ends, outer, middle, mine, other, tail):
    first = lax.axis_index("dp") == 0
    inner = inner_chip()
    rows, part = mine.shape
    step = chunk_of(part, 512)

    def total(columns):
        near = jnp.where(inner, 0.0, ends[:, columns].astype(f32))
        value = own[:, columns].astype(f32) + far[:, columns].astype(f32) + near
        value = value + outer[:, columns].astype(f32) + middle[:, columns].astype(f32)
        top, low = value[:rows], value[rows:]
        return jnp.where(first, top, low), jnp.where(first, low, top)

    def body(k, carry):
        columns = pl.ds(pl.multiple_of(k * step, 128), step)
        here, there = total(columns)
        mine[:, columns] = here.astype(bf16)
        other[:, columns] = there.astype(bf16)
        return carry

    lax.fori_loop(0, part // step, body, 0)
    tail[...] = total(slice(part, part + 128))[0]


def step_of(part, split):
    for step in (512, 256):
        if part % step == 0 and split % step == 0:
            return step
    return 128


def row_specs(count, step, half):
    spec = pl.BlockSpec((count, step), lambda i: (half, i))
    return [spec] * 5


def piece_specs(step, split, wide):
    upper = split // step
    whole = pl.BlockSpec((step, wide), lambda i: (i, 0))
    top = pl.BlockSpec((step, wide), lambda i: (jnp.minimum(i, upper - 1), 0))
    low = pl.BlockSpec((step, wide), lambda i: (jnp.maximum(i - upper, 0), 0))
    return [whole, whole, top, low, top, low]


def piece_blocks(pieces, upper):
    here = pl.program_id(0) < upper
    first, second, top2, low2, top3, low3 = [p[...] for p in pieces]
    return [first, second, jnp.where(here, top2, low2), jnp.where(here, top3, low3)]


def gate_up_kernel(upper, *refs):
    blocks, pieces, out = refs[:5], refs[5:-1], refs[-1]
    wide = pieces[0].shape[1]

    @pl.when(pl.program_id(0) == 0)
    def _():
        out[...] = jnp.zeros_like(out)

    x = slot_rows(blocks)
    for q, w in enumerate(piece_blocks(pieces, upper)):
        out[:, q * wide : (q + 1) * wide] += jnp.dot(x, w, preferred_element_type=f32)


def proj_kernel(*refs):
    blocks, pieces, out = refs[:5], refs[5:-1], refs[-1]
    rows, wide = pieces[0].shape
    ff = wide // 2

    @pl.when(pl.program_id(0) == 0)
    def _():
        out[...] = jnp.zeros_like(out)

    c = slot_rows(blocks)
    w = jnp.concatenate(
        [
            jnp.concatenate([p[at : at + ff, :] for at in range(0, rows, ff)], axis=1)
            for p in pieces
        ],
        axis=0,
    )
    out[...] += lax.dot_general(c, w, CONTRACT1, preferred_element_type=f32)


def activations(mine, theirs, q, ff):
    base = 2 * q * ff
    g = mine[:, base : base + ff] + theirs[:, base : base + ff]
    u = mine[:, base + ff : base + 2 * ff] + theirs[:, base + ff : base + 2 * ff]
    sig = jax.nn.sigmoid(g)
    return g, u, sig, g * sig


def down_kernel(mine, theirs, *refs):
    blocks, outs, scratch = refs[:5], refs[5:-1], refs[-1]
    own, sent1, sent2, kept1, kept2 = outs
    ff = own.shape[0]
    half = ff // 2
    step = blocks[0].shape[1]

    @pl.when(pl.program_id(0) == 0)
    def _():
        for q in range(QUAD):
            g, u, sig, active = activations(mine, theirs, q, ff)
            hidden = (active * u).astype(bf16).astype(f32)
            scratch[q * ff : (q + 1) * ff, :] = hidden.T.astype(bf16)

    columns = pl.ds(pl.multiple_of(pl.program_id(0) * step, 128), step)
    rows = slot_rows(blocks)
    grads = jnp.dot(scratch[...], rows, preferred_element_type=f32).astype(bf16)
    g0, g1, g2, g3 = [grads[q * ff : (q + 1) * ff] for q in range(QUAD)]
    own[:, columns] = g0
    sent1[:, columns] = jnp.concatenate([g3[:half], g1[:half]], axis=0)
    sent2[:, columns] = jnp.concatenate([g3[half:], g2[half:]], axis=0)
    kept1[:, columns] = g1[half:]
    kept2[:, columns] = g2[:half]


def back_kernel(upper, mine, theirs, proj_mine, proj_theirs, *refs):
    members = SPLIT // QUAD
    pieces, outs, scratch = refs[: -members - 1], refs[-members - 1 : -1], refs[-1]
    step, wide = pieces[0].shape
    ff = wide // 2
    rows = outs[0].shape[0]
    part = outs[0].shape[1] - 128

    @pl.when(pl.program_id(0) == 0)
    def _():
        dots = 0.0
        for q in range(QUAD):
            g, u, sig, active = activations(mine, theirs, q, ff)
            proj = proj_mine[:, q * ff : (q + 1) * ff] + proj_theirs[:, q * ff : (q + 1) * ff]
            hidden = (active * u).astype(bf16).astype(f32)
            dots = dots + jnp.sum(hidden * proj, axis=1, keepdims=True)
            base = 2 * q * ff
            dgate = proj * u * sig * (1.0 + g * (1.0 - sig))
            scratch[:, base : base + ff] = dgate.astype(bf16)
            scratch[:, base + ff : base + 2 * ff] = (proj * active).astype(bf16)

        high = dots.astype(bf16).astype(f32)
        rest = dots - high
        lane = lax.broadcasted_iota(jnp.int32, (rows, 128), 1)
        for i, out in enumerate(outs):
            at = 2 if i == 2 else 0
            top, low = high[i * rows : (i + 1) * rows], rest[i * rows : (i + 1) * rows]
            out[:, part : part + 128] = jnp.where(
                lane == at, top, jnp.where(lane == at + 1, low, 0.0)
            ).astype(bf16)

    columns = pl.ds(pl.multiple_of(pl.program_id(0) * step, 128), step)
    w = jnp.concatenate(piece_blocks(pieces, upper), axis=1)
    grads = lax.dot_general(scratch[...], w, CONTRACT1, preferred_element_type=f32)
    for i, out in enumerate(outs):
        out[:, columns] = grads[i * rows : (i + 1) * rows].astype(bf16)


def final_kernel(held, pick, mine, theirs, tail, chosen, inv_w, inv_total, mark, tok_out, logit_out):
    core = lax.axis_index("dp")
    slots, part = mine.shape
    step = chunk_of(part, 512)
    pick_t = pick[...]

    def body(k, carry):
        at = pl.multiple_of(k * step, 128)
        for source, side in ((mine, core), (theirs, 1 - core)):
            block = lax.dot_general(
                pick_t, source[:, pl.ds(at, step)], CONTRACT0, preferred_element_type=f32
            )
            tok_out[:, pl.ds(pl.multiple_of(side * part + at, 128), step)] = block.astype(bf16)
        return carry

    lax.fori_loop(0, part // step, body, 0)
    values = jnp.sum(tail[...], axis=1, keepdims=True)
    entries = pick_t.astype(f32) * values
    full = chosen.shape
    expert = lax.broadcasted_iota(jnp.int32, full, 0)
    slot = lax.broadcasted_iota(jnp.int32, entries.shape, 0)
    capacity = slots // held
    dw = jnp.zeros(full, f32)
    for e in range(held):
        inside = (slot >= e * capacity) & (slot < (e + 1) * capacity)
        found = jnp.sum(jnp.where(inside, entries, 0.0), axis=0, keepdims=True)
        dw = jnp.where(expert == e, jnp.broadcast_to(found, full), dw)
    dw = dw * inv_w[...]
    share = chosen[...]
    inner = jnp.sum(dw * share, axis=0, keepdims=True) * inv_total[...]
    logit_out[...] = SCALE * inv_total[...] * (dw - inner) * share * (1.0 - share)


def call(kernel, outs, in_specs, scratch, flops, moved, limit=20, out_specs=None, grid=()):
    return pl.pallas_call(
        kernel,
        out_shape=outs,
        grid=grid,
        in_specs=in_specs,
        out_specs=out_specs or [VMEM] * len(outs),
        scratch_shapes=scratch,
        compiler_params=pltpu.CompilerParams(vmem_limit_bytes=limit * 1024 * 1024),
        cost_estimate=pl.CostEstimate(flops=flops, bytes_accessed=moved, transcendentals=0),
    )


def per_device(tokens, cotangent, logits, expert_ids, gate_proj, up_proj, down_proj):
    devices = lax.axis_size("expert")
    cores = lax.axis_size("dp")
    core = lax.axis_index("dp")
    held = devices // SPLIT
    tok_count, top = expert_ids.shape
    experts = logits.shape[1]
    width = tokens.shape[1]
    ff = gate_proj.shape[2]
    part = width // cores
    capacity = max(2, 5 * tok_count * top // (4 * experts))
    members = SPLIT // QUAD
    rows_dev = held * capacity
    rows_chip = cores * rows_dev
    slots = members * rows_chip
    across = [[e * SPLIT + j for e in range(held)] for j in range(SPLIT)]
    swap1 = [(i, i ^ 1) for i in range(devices)]
    swap2 = [(i, i ^ 2) for i in range(devices)]
    sibling = [(c, cores - 1 - c) for c in range(cores)]
    barrier = lax.optimization_barrier

    def send(array, route):
        return lax.ppermute(array, "expert", route)

    def line(pairs):
        return [
            (e * SPLIT + a * QUAD + q, e * SPLIT + b * QUAD + q)
            for e in range(held)
            for a, b in pairs
            for q in range(QUAD)
        ]

    distant = line([(m, m ^ 2) for m in range(members)])
    outward = line([(1, 0), (2, 3)])
    inward = line([(0, 1), (3, 2)])
    middle_swap = line([(1, 2), (2, 1)])
    inner = inner_chip()

    lowf = ff // 2
    packed = part + part // 2
    split = split_of(packed)
    shape = jax.ShapeDtypeStruct
    hbm = pl.BlockSpec(memory_space=pltpu.HBM)
    weights, w_top, w_low = call(
        pack_kernel,
        [shape((size, 2 * ff), bf16) for size in (packed, split, packed - split)],
        [hbm] * 3,
        [pltpu.VMEM((packed, 2 * ff), bf16), pltpu.SemaphoreType.DMA((5 + part // (2 * ff),))],
        0,
        12 * part * ff,
        limit=58,
        out_specs=[hbm] * 3,
    )(gate_proj, up_proj, down_proj)
    weights, w_top, w_low, logits, tokens = barrier((weights, w_top, w_low, logits, tokens))
    mine, other, pick, chosen, inv_w, inv_total = call(
        lambda *refs: prep_kernel(held, capacity, *refs),
        [shape((2, rows_dev, part), bf16)] * 2
        + [shape((rows_dev, tok_count), bf16)]
        + [shape((experts, tok_count), f32)] * 3,
        [VMEM] * 4,
        [],
        4 * rows_dev * tok_count * width,
        4 * tok_count * width,
        limit=58,
    )(tokens, cotangent, logits.T, expert_ids.T)
    w1 = send(weights, swap1)
    w2_top = send(w_top, swap2)
    w2_low = send(w_low, swap2)

    theirs = lax.ppermute(other, "dp", sibling)
    own = jnp.concatenate(
        [
            jnp.where(core == (0 if side == 0 else cores - 1), mine[i], theirs[i])
            for i in range(2)
            for side in range(cores)
        ],
        axis=0,
    )
    if held > 1:
        own = own.reshape(2, cores, held, capacity, part)
        own = lax.all_to_all(own, "expert", 2, 2, axis_index_groups=across, tiled=True)
        own = own.reshape(2 * rows_chip, part)
    far = send(own, distant)
    outer = send(own, outward)
    (mark,) = call(
        arrived_kernel,
        [shape((8, 128), f32)],
        [pl.BlockSpec(memory_space=pl.ANY)] * 3,
        [],
        8 * slots * part * QUAD * ff * 8,
        0,
    )(w1, w2_top, w2_low)
    w1, w2_top, w2_low, own, far, outer, mark = barrier(
        (w1, w2_top, w2_low, own, far, outer, mark)
    )
    w3_top = send(w2_top, swap1)
    w3_low = send(w1[split:], swap2)
    ends = send(jnp.where(inner, far, own), outward + inward)
    middle = send(own, middle_swap)
    w = [weights, w1, w2_top, w2_low, w3_top, w3_low]
    blocks = [own, far, ends, outer, middle]

    matmul = 2 * slots * part * QUAD * ff
    step = step_of(part, split)
    upper = split // step
    grid = (part // step,)
    w_specs = piece_specs(step, split, 2 * ff)
    (g_u,) = call(
        lambda *refs: gate_up_kernel(upper, *refs),
        [shape((slots, QUAD * 2 * ff), f32)],
        row_specs(rows_chip, step, 0) + w_specs,
        [],
        2 * matmul,
        2 * part * (slots + QUAD * 2 * ff),
        grid=grid,
    )(*blocks, *w)
    g_u_sib = lax.ppermute(g_u, "dp", sibling)
    half = step // 2
    in_whole = pl.BlockSpec((half, 2 * ff), lambda i: (part // half + i, 0))
    in_low = pl.BlockSpec((half, 2 * ff), lambda i: ((part - split) // half + i, 0))
    (proj,) = call(
        proj_kernel,
        [shape((slots, QUAD * ff), f32)],
        row_specs(rows_chip, step, 1) + [in_whole, in_whole, in_low, in_low],
        [],
        matmul,
        2 * part * (slots + QUAD * ff),
        grid=grid,
    )(*blocks, weights, w1, w2_low, w3_low)
    proj_sib = lax.ppermute(proj, "dp", sibling)
    g0, sent1, sent2, kept1, kept2 = call(
        down_kernel,
        [shape((ff, part), bf16)] * 3 + [shape((lowf, part), bf16)] * 2,
        [VMEM] * 2 + row_specs(rows_chip, step, 1),
        [pltpu.VMEM((QUAD * ff, slots), bf16)],
        matmul,
        2 * part * (slots + QUAD * ff),
        grid=grid,
    )(g_u, g_u_sib, *blocks)
    g0, sent1, sent2, proj, proj_sib = barrier((g0, sent1, sent2, proj, proj_sib))
    got1 = send(sent1, swap1)
    got2 = send(sent2, swap2)
    b0, b1, b2, b3 = call(
        lambda *refs: back_kernel(upper, *refs),
        [shape((rows_chip, part + 128), bf16)] * members,
        [VMEM] * 4 + w_specs,
        [pltpu.VMEM((slots, QUAD * 2 * ff), bf16)],
        2 * matmul,
        2 * part * (slots + QUAD * 2 * ff),
        grid=grid,
    )(g_u, g_u_sib, proj, proj_sib, *w)

    ends = send(b2, outward + inward)
    middle = send(b3, middle_swap)
    ends, middle, got1, got2, b1, b3 = barrier((ends, middle, got1, got2, b1, b3))
    joined = b1 + jnp.where(inner, ends, jnp.zeros((), bf16))
    joined, got1, got2 = barrier((joined, got1, got2))
    far = send(joined, distant)
    outer = send(b3, inward)
    got3 = send(kept1 + got2[:lowf], swap1)
    got4 = send(kept2 + got1[:lowf], swap2)
    mine, other, tail = call(
        sum_kernel,
        [shape((rows_dev, part), bf16)] * 2 + [shape((rows_dev, 128), f32)],
        [VMEM] * 5,
        [],
        matmul,
        12 * rows_chip * part,
    )(b0, far, ends, outer, middle)
    other, got3, got4 = barrier((other, got3, got4))
    add = lambda a, b, c: (a.astype(f32) + b.astype(f32) + c.astype(f32)).astype(bf16)
    down_grad = jnp.concatenate(
        [add(g0[:lowf], got1[lowf:], got4), add(g0[lowf:], got2[lowf:], got3)], axis=0
    )[None]
    if held > 1:
        mine, other, tail = [
            lax.all_to_all(
                array.reshape(held, capacity, array.shape[1]),
                "expert",
                0,
                0,
                axis_index_groups=across,
                tiled=True,
            ).reshape(array.shape)
            for array in (mine, other, tail)
        ]
    theirs = lax.ppermute(other, "dp", sibling)
    token_grad, logit_grad = call(
        lambda *refs: final_kernel(held, *refs),
        [
            shape((tok_count, width), bf16),
            shape((experts, tok_count), f32),
        ],
        [VMEM] * 8,
        [],
        2 * tok_count * rows_dev * width,
        2 * width * (tok_count + rows_dev),
    )(pick, mine, theirs, tail, chosen, inv_w, inv_total, mark)
    return (token_grad, logit_grad.T, down_grad)


def solution(mesh):
    in_specs = (
        P(("expert", "dp"), None),
        P(("expert", "dp"), None),
        P(("expert", "dp"), None),
        P(("expert", "dp"), None),
        P("expert", None, None),
        P("expert", None, None),
        P("expert", None, None),
    )
    out_specs = (P(("expert", "dp"), None), P(("expert", "dp"), None), P("expert", None, "dp"))
    return jax.shard_map(
        per_device, mesh=mesh, in_specs=in_specs, out_specs=out_specs, check_vma=False
    )
```

```python
import jax
import jax.numpy as jnp
from jax import lax
from jax.experimental import pallas as pl
from jax.experimental.pallas import tpu as pltpu
from jax.sharding import PartitionSpec as P

SPLIT = 16
SCALE = 2.5
QUAD = 4
bf16 = jnp.bfloat16
f32 = jnp.float32
CONTRACT0 = (((0,), (0,)), ((), ()))
CONTRACT1 = (((1,), (1,)), ((), ()))
VMEM = pl.BlockSpec(memory_space=pltpu.VMEM)


def chunk_of(size, limit):
    best = 128
    for step in range(128, limit + 1, 128):
        if size % step == 0:
            best = step
    return best


def inner_chip():
    member = lax.rem(lax.axis_index("expert"), SPLIT) // QUAD
    return (member > 0) & (member < SPLIT // QUAD - 1)


def slot_rows(blocks):
    own, far, ends, outer, middle = [b[...] for b in blocks]
    return jnp.concatenate([own, far, ends, jnp.where(inner_chip(), middle, outer)], axis=0)


def split_of(total):
    return total // 2 // 256 * 256


def pack_kernel(gate, up, down, weights, packed, sems):
    ff = gate.shape[2]
    wide = 2 * ff
    part = packed.shape[0] * 2 // 3
    start = pl.multiple_of(lax.axis_index("dp") * part, 128)
    half = pl.ds(start, part)
    pairs = [
        (gate.at[0, half, :], packed.at[:part, :ff]),
        (up.at[0, half, :], packed.at[:part, ff:]),
    ]
    for c in range(part // wide):
        columns = pl.ds(pl.multiple_of(start + c * wide, 128), wide)
        pairs.append((down.at[0, :, columns], packed.at[part + c * ff : part + (c + 1) * ff, :]))
    reads = len(pairs)
    pairs.append((packed, weights))
    copies = [
        pltpu.make_async_copy(src, dst, sems.at[i]) for i, (src, dst) in enumerate(pairs)
    ]
    for copy in copies[:reads]:
        copy.start()
    for copy in copies[:reads]:
        copy.wait()
    for copy in copies[reads:]:
        copy.start()
    for copy in copies[reads:]:
        copy.wait()


def arrived_kernel(w1, w2, mark):
    mark[...] = jnp.zeros_like(mark)


def prep_kernel(held, capacity, *refs):
    tokens, cotangent, logits, ids = refs[:4]
    mine, other, pick_out, chosen_out, inv_w_out, inv_total_out = refs[4:]
    part = mine.shape[2]
    core = lax.axis_index("dp")
    start = pl.multiple_of(core * part, 128)
    away = pl.multiple_of((1 - core) * part, 128)

    experts, count = logits.shape
    expert = lax.broadcasted_iota(jnp.int32, (experts, count), 0)
    has = expert == ids[0:1, :]
    for k in range(1, ids.shape[0]):
        has = has | (expert == ids[k : k + 1, :])
    chosen = jnp.where(has, jax.nn.sigmoid(logits[...]), 0.0)
    total = jnp.sum(chosen, axis=0, keepdims=True)
    weight = (SCALE * chosen / total).astype(bf16).astype(f32)
    before = lax.broadcasted_iota(jnp.int32, (count, count), 0)
    after = lax.broadcasted_iota(jnp.int32, (count, count), 1)
    earlier = jnp.where(before < after, 1.0, 0.0).astype(bf16)
    named = jnp.where(has, 1.0, 0.0)
    rank = jnp.dot(named.astype(bf16), earlier, preferred_element_type=f32)
    slots = held * capacity
    slot = lax.broadcasted_iota(jnp.int32, (slots, count), 0)
    pick = jnp.zeros((slots, count), f32)
    value = jnp.zeros((slots, count), f32)
    for e in range(held):
        place = rank[e : e + 1, :].astype(jnp.int32) + e * capacity
        hit = jnp.where(slot == place, named[e : e + 1, :], 0.0)
        pick = pick + hit
        value = value + hit * weight[e : e + 1, :]
    value = jnp.sum(value, axis=1, keepdims=True)
    pick = pick.astype(bf16)
    pick_out[...] = pick
    chosen_out[...] = chosen
    inv_w_out[...] = jnp.where(has & (expert < held), 1.0 / weight, 0.0)
    inv_total_out[...] = jnp.broadcast_to(1.0 / total, chosen.shape)

    step = chunk_of(part, 512)

    def body(k, carry):
        at = pl.multiple_of(k * step, 128)
        for base, out in ((start, mine), (away, other)):
            columns = pl.ds(pl.multiple_of(base + at, 128), step)
            x = jnp.dot(pick, tokens[:, columns], preferred_element_type=f32)
            c = jnp.dot(pick, cotangent[:, columns], preferred_element_type=f32)
            out[0, :, pl.ds(at, step)] = x.astype(bf16)
            out[1, :, pl.ds(at, step)] = (c * value).astype(bf16)
        return carry

    lax.fori_loop(0, part // step, body, 0)


def sum_kernel(own, far, ends, outer, middle, mine, other, tail):
    first = lax.axis_index("dp") == 0
    inner = inner_chip()
    rows, part = mine.shape
    step = chunk_of(part, 512)

    def total(columns):
        near = jnp.where(inner, 0.0, ends[:, columns].astype(f32))
        value = own[:, columns].astype(f32) + far[:, columns].astype(f32) + near
        value = value + outer[:, columns].astype(f32) + middle[:, columns].astype(f32)
        top, low = value[:rows], value[rows:]
        return jnp.where(first, top, low), jnp.where(first, low, top)

    def body(k, carry):
        columns = pl.ds(pl.multiple_of(k * step, 128), step)
        here, there = total(columns)
        mine[:, columns] = here.astype(bf16)
        other[:, columns] = there.astype(bf16)
        return carry

    lax.fori_loop(0, part // step, body, 0)
    tail[...] = total(slice(part, part + 128))[0]


def step_of(part, split):
    for step in (512, 256):
        if part % step == 0 and split % step == 0:
            return step
    return 128


def row_specs(count, step, half):
    spec = pl.BlockSpec((count, step), lambda i: (half, i))
    return [spec] * 5


def piece_specs(step, split, wide):
    upper = split // step
    whole = pl.BlockSpec((step, wide), lambda i: (i, 0))
    top = pl.BlockSpec((step, wide), lambda i: (jnp.minimum(i, upper - 1), 0))
    low = pl.BlockSpec((step, wide), lambda i: (jnp.maximum(i - upper, 0), 0))
    return [whole, whole, whole, top, low]


def piece_blocks(pieces, upper):
    here = pl.program_id(0) < upper
    *whole, top, low = [p[...] for p in pieces]
    return whole + [jnp.where(here, top, low)]


def fetch_rows(blocks, first, rows, either, sems):
    own, far, ends, outer, middle = blocks
    count = either.shape[1]
    take = slice(first, first + count)
    targets = [rows.at[i * count : (i + 1) * count, :] for i in range(3)]
    targets += [either.at[0], either.at[1]]
    return [
        pltpu.make_async_copy(src.at[take, :], dst, sems.at[i])
        for i, (src, dst) in enumerate(zip((own, far, ends, outer, middle), targets))
    ]


def finish_rows(copies, rows, either):
    for copy in copies:
        copy.wait()
    count = either.shape[1]
    rows[3 * count :, :] = jnp.where(inner_chip(), either[1], either[0])


def gate_up_kernel(*refs):
    blocks, pieces, (out, rows, either, buffer, sems) = refs[:5], refs[5:10], refs[10:]
    *whole, top, low = pieces
    part, wide = buffer.shape[1:]
    split = top.shape[0]
    loads = fetch_rows(blocks, 0, rows, either, sems)
    pairs = [(p.at[:part, :], buffer.at[q]) for q, p in enumerate(whole)]
    pairs.append((top, buffer.at[3, :split, :]))
    pairs.append((low.at[: part - split, :], buffer.at[3, split:, :]))
    copies = [
        pltpu.make_async_copy(src, dst, sems.at[5 + i]) for i, (src, dst) in enumerate(pairs)
    ]
    for copy in loads + copies:
        copy.start()
    finish_rows(loads, rows, either)
    for q, needed in enumerate((copies[:1], copies[1:2], copies[2:3], copies[3:])):
        for copy in needed:
            copy.wait()
        out[:, q * wide : (q + 1) * wide] = jnp.dot(
            rows[...], buffer[q], preferred_element_type=f32
        )


def proj_kernel(*refs):
    blocks, pieces, (out, rows, either, buffer, sems) = refs[:5], refs[5:9], refs[9:]
    height, wide = buffer.shape[1:]
    ff = wide // 2
    count = either.shape[1]
    loads = fetch_rows(blocks, count, rows, either, sems)
    copies = [
        pltpu.make_async_copy(p.at[p.shape[0] - height :, :], buffer.at[q], sems.at[5 + q])
        for q, p in enumerate(pieces)
    ]
    for copy in loads + copies:
        copy.start()
    finish_rows(loads, rows, either)
    for q in range(0, QUAD, 2):
        for copy in copies[q : q + 2]:
            copy.wait()
        w = jnp.concatenate(
            [
                jnp.concatenate(
                    [buffer[i, at : at + ff, :] for at in range(0, height, ff)], axis=1
                )
                for i in (q, q + 1)
            ],
            axis=0,
        )
        out[:, q * ff : (q + 2) * ff] = lax.dot_general(
            rows[...], w, CONTRACT1, preferred_element_type=f32
        )


def activations(mine, theirs, q, ff):
    base = 2 * q * ff
    g = mine[:, base : base + ff] + theirs[:, base : base + ff]
    u = mine[:, base + ff : base + 2 * ff] + theirs[:, base + ff : base + 2 * ff]
    sig = jax.nn.sigmoid(g)
    return g, u, sig, g * sig


def down_kernel(mine, theirs, *refs):
    blocks, outs, scratch = refs[:5], refs[5:-1], refs[-1]
    own, sent1, sent2, kept1, kept2 = outs
    ff = own.shape[0]
    half = ff // 2
    step = blocks[0].shape[1]

    @pl.when(pl.program_id(0) == 0)
    def _():
        for q in range(QUAD):
            g, u, sig, active = activations(mine, theirs, q, ff)
            hidden = (active * u).astype(bf16).astype(f32)
            scratch[q * ff : (q + 1) * ff, :] = hidden.T.astype(bf16)

    columns = pl.ds(pl.multiple_of(pl.program_id(0) * step, 128), step)
    rows = slot_rows(blocks)
    grads = jnp.dot(scratch[...], rows, preferred_element_type=f32).astype(bf16)
    g0, g1, g2, g3 = [grads[q * ff : (q + 1) * ff] for q in range(QUAD)]
    own[:, columns] = g0
    sent1[:, columns] = jnp.concatenate([g3[:half], g1[:half]], axis=0)
    sent2[:, columns] = jnp.concatenate([g3[half:], g2[half:]], axis=0)
    kept1[:, columns] = g1[half:]
    kept2[:, columns] = g2[:half]


def back_kernel(upper, mine, theirs, proj_mine, proj_theirs, *refs):
    members = SPLIT // QUAD
    pieces, outs, scratch = refs[: -members - 1], refs[-members - 1 : -1], refs[-1]
    step, wide = pieces[0].shape
    ff = wide // 2
    rows = outs[0].shape[0]
    part = outs[0].shape[1] - 128

    @pl.when(pl.program_id(0) == 0)
    def _():
        dots = 0.0
        for q in range(QUAD):
            g, u, sig, active = activations(mine, theirs, q, ff)
            proj = proj_mine[:, q * ff : (q + 1) * ff] + proj_theirs[:, q * ff : (q + 1) * ff]
            hidden = (active * u).astype(bf16).astype(f32)
            dots = dots + jnp.sum(hidden * proj, axis=1, keepdims=True)
            base = 2 * q * ff
            dgate = proj * u * sig * (1.0 + g * (1.0 - sig))
            scratch[:, base : base + ff] = dgate.astype(bf16)
            scratch[:, base + ff : base + 2 * ff] = (proj * active).astype(bf16)

        high = dots.astype(bf16).astype(f32)
        rest = dots - high
        lane = lax.broadcasted_iota(jnp.int32, (rows, 128), 1)
        for i, out in enumerate(outs):
            at = 2 if i == 2 else 0
            top, low = high[i * rows : (i + 1) * rows], rest[i * rows : (i + 1) * rows]
            out[:, part : part + 128] = jnp.where(
                lane == at, top, jnp.where(lane == at + 1, low, 0.0)
            ).astype(bf16)

    columns = pl.ds(pl.multiple_of(pl.program_id(0) * step, 128), step)
    w = jnp.concatenate(piece_blocks(pieces, upper), axis=1)
    grads = lax.dot_general(scratch[...], w, CONTRACT1, preferred_element_type=f32)
    for i, out in enumerate(outs):
        out[:, columns] = grads[i * rows : (i + 1) * rows].astype(bf16)


def final_kernel(held, pick, mine, theirs, tail, chosen, inv_w, inv_total, mark, tok_out, logit_out):
    core = lax.axis_index("dp")
    slots, part = mine.shape
    step = chunk_of(part, 512)
    pick_t = pick[...]

    def body(k, carry):
        at = pl.multiple_of(k * step, 128)
        for source, side in ((mine, core), (theirs, 1 - core)):
            block = lax.dot_general(
                pick_t, source[:, pl.ds(at, step)], CONTRACT0, preferred_element_type=f32
            )
            tok_out[:, pl.ds(pl.multiple_of(side * part + at, 128), step)] = block.astype(bf16)
        return carry

    lax.fori_loop(0, part // step, body, 0)
    values = jnp.sum(tail[...], axis=1, keepdims=True)
    entries = pick_t.astype(f32) * values
    full = chosen.shape
    expert = lax.broadcasted_iota(jnp.int32, full, 0)
    slot = lax.broadcasted_iota(jnp.int32, entries.shape, 0)
    capacity = slots // held
    dw = jnp.zeros(full, f32)
    for e in range(held):
        inside = (slot >= e * capacity) & (slot < (e + 1) * capacity)
        found = jnp.sum(jnp.where(inside, entries, 0.0), axis=0, keepdims=True)
        dw = jnp.where(expert == e, jnp.broadcast_to(found, full), dw)
    dw = dw * inv_w[...]
    share = chosen[...]
    inner = jnp.sum(dw * share, axis=0, keepdims=True) * inv_total[...]
    logit_out[...] = SCALE * inv_total[...] * (dw - inner) * share * (1.0 - share)


def call(kernel, outs, in_specs, scratch, flops, moved, limit=20, out_specs=None, grid=()):
    return pl.pallas_call(
        kernel,
        out_shape=outs,
        grid=grid,
        in_specs=in_specs,
        out_specs=out_specs or [VMEM] * len(outs),
        scratch_shapes=scratch,
        compiler_params=pltpu.CompilerParams(vmem_limit_bytes=limit * 1024 * 1024),
        cost_estimate=pl.CostEstimate(flops=flops, bytes_accessed=moved, transcendentals=0),
    )


def per_device(tokens, cotangent, logits, expert_ids, gate_proj, up_proj, down_proj):
    devices = lax.axis_size("expert")
    cores = lax.axis_size("dp")
    core = lax.axis_index("dp")
    held = devices // SPLIT
    tok_count, top = expert_ids.shape
    experts = logits.shape[1]
    width = tokens.shape[1]
    ff = gate_proj.shape[2]
    part = width // cores
    capacity = max(2, 5 * tok_count * top // (4 * experts))
    members = SPLIT // QUAD
    rows_dev = held * capacity
    rows_chip = cores * rows_dev
    slots = members * rows_chip
    across = [[e * SPLIT + j for e in range(held)] for j in range(SPLIT)]
    swap1 = [(i, i ^ 1) for i in range(devices)]
    swap2 = [(i, i ^ 2) for i in range(devices)]
    sibling = [(c, cores - 1 - c) for c in range(cores)]
    barrier = lax.optimization_barrier

    def send(array, route):
        return lax.ppermute(array, "expert", route)

    def line(pairs):
        return [
            (e * SPLIT + a * QUAD + q, e * SPLIT + b * QUAD + q)
            for e in range(held)
            for a, b in pairs
            for q in range(QUAD)
        ]

    distant = line([(m, m ^ 2) for m in range(members)])
    outward = line([(1, 0), (2, 3)])
    inward = line([(0, 1), (3, 2)])
    middle_swap = line([(1, 2), (2, 1)])
    inner = inner_chip()

    lowf = ff // 2
    packed = part + part // 2
    split = split_of(packed)
    shape = jax.ShapeDtypeStruct
    hbm = pl.BlockSpec(memory_space=pltpu.HBM)
    (weights,) = call(
        pack_kernel,
        [shape((packed, 2 * ff), bf16)],
        [hbm] * 3,
        [pltpu.VMEM((packed, 2 * ff), bf16), pltpu.SemaphoreType.DMA((3 + part // (2 * ff),))],
        0,
        12 * part * ff,
        limit=58,
        out_specs=[hbm],
    )(gate_proj, up_proj, down_proj)
    weights, logits, tokens = barrier((weights, logits, tokens))
    mine, other, pick, chosen, inv_w, inv_total = call(
        lambda *refs: prep_kernel(held, capacity, *refs),
        [shape((2, rows_dev, part), bf16)] * 2
        + [shape((rows_dev, tok_count), bf16)]
        + [shape((experts, tok_count), f32)] * 3,
        [VMEM] * 4,
        [],
        4 * rows_dev * tok_count * width,
        4 * tok_count * width,
        limit=58,
    )(tokens, cotangent, logits.T, expert_ids.T)
    w1 = send(weights, swap1)
    w2 = send(weights, swap2)

    theirs = lax.ppermute(other, "dp", sibling)
    own = jnp.concatenate(
        [
            jnp.where(core == (0 if side == 0 else cores - 1), mine[i], theirs[i])
            for i in range(2)
            for side in range(cores)
        ],
        axis=0,
    )
    if held > 1:
        own = own.reshape(2, cores, held, capacity, part)
        own = lax.all_to_all(own, "expert", 2, 2, axis_index_groups=across, tiled=True)
        own = own.reshape(2 * rows_chip, part)
    far = send(own, distant)
    outer = send(own, outward)
    (mark,) = call(
        arrived_kernel,
        [shape((8, 128), f32)],
        [pl.BlockSpec(memory_space=pl.ANY)] * 2,
        [],
        64 * slots * part * QUAD * ff,
        0,
    )(w1, w2)
    w1, w2, own, far, outer, mark = barrier((w1, w2, own, far, outer, mark))
    w3_top = send(w2[:split], swap1)
    w3_low = send(w1[split:], swap2)
    ends = send(jnp.where(inner, far, own), outward + inward)
    middle = send(own, middle_swap)
    w = [weights, w1, w2, w3_top, w3_low]
    blocks = [own, far, ends, outer, middle]

    matmul = 2 * slots * part * QUAD * ff
    step = step_of(part, split)
    upper = split // step
    grid = (part // step,)
    w_specs = piece_specs(step, split, 2 * ff)
    anywhere = pl.BlockSpec(memory_space=pl.ANY)
    row_scratch = [
        pltpu.VMEM((slots, part), bf16),
        pltpu.VMEM((2, rows_chip, part), bf16),
    ]
    (g_u,) = call(
        gate_up_kernel,
        [shape((slots, QUAD * 2 * ff), f32)],
        [anywhere] * 10,
        row_scratch + [pltpu.VMEM((QUAD, part, 2 * ff), bf16), pltpu.SemaphoreType.DMA((10,))],
        2 * matmul,
        2 * part * (slots + QUAD * 2 * ff),
    )(*blocks, *w)
    g_u_sib = lax.ppermute(g_u, "dp", sibling)
    (proj,) = call(
        proj_kernel,
        [shape((slots, QUAD * ff), f32)],
        [anywhere] * 9,
        row_scratch + [pltpu.VMEM((QUAD, part // 2, 2 * ff), bf16), pltpu.SemaphoreType.DMA((9,))],
        matmul,
        2 * part * (slots + QUAD * ff),
    )(*blocks, weights, w1, w2, w3_low)
    proj_sib = lax.ppermute(proj, "dp", sibling)
    g0, sent1, sent2, kept1, kept2 = call(
        down_kernel,
        [shape((ff, part), bf16)] * 3 + [shape((lowf, part), bf16)] * 2,
        [VMEM] * 2 + row_specs(rows_chip, step, 1),
        [pltpu.VMEM((QUAD * ff, slots), bf16)],
        matmul,
        2 * part * (slots + QUAD * ff),
        grid=grid,
    )(g_u, g_u_sib, *blocks)
    g0, sent1, sent2, proj, proj_sib = barrier((g0, sent1, sent2, proj, proj_sib))
    got1 = send(sent1, swap1)
    got2 = send(sent2, swap2)
    b0, b1, b2, b3 = call(
        lambda *refs: back_kernel(upper, *refs),
        [shape((rows_chip, part + 128), bf16)] * members,
        [VMEM] * 4 + w_specs,
        [pltpu.VMEM((slots, QUAD * 2 * ff), bf16)],
        2 * matmul,
        2 * part * (slots + QUAD * 2 * ff),
        grid=grid,
    )(g_u, g_u_sib, proj, proj_sib, *w)

    ends = send(b2, outward + inward)
    middle = send(b3, middle_swap)
    ends, middle, got1, got2, b1, b3 = barrier((ends, middle, got1, got2, b1, b3))
    joined = b1 + jnp.where(inner, ends, jnp.zeros((), bf16))
    joined, got1, got2 = barrier((joined, got1, got2))
    far = send(joined, distant)
    outer = send(b3, inward)
    got3 = send(kept1 + got2[:lowf], swap1)
    got4 = send(kept2 + got1[:lowf], swap2)
    mine, other, tail = call(
        sum_kernel,
        [shape((rows_dev, part), bf16)] * 2 + [shape((rows_dev, 128), f32)],
        [VMEM] * 5,
        [],
        matmul,
        12 * rows_chip * part,
    )(b0, far, ends, outer, middle)
    other, got3, got4 = barrier((other, got3, got4))
    add = lambda a, b, c: (a.astype(f32) + b.astype(f32) + c.astype(f32)).astype(bf16)
    down_grad = jnp.concatenate(
        [add(g0[:lowf], got1[lowf:], got4), add(g0[lowf:], got2[lowf:], got3)], axis=0
    )[None]
    if held > 1:
        mine, other, tail = [
            lax.all_to_all(
                array.reshape(held, capacity, array.shape[1]),
                "expert",
                0,
                0,
                axis_index_groups=across,
                tiled=True,
            ).reshape(array.shape)
            for array in (mine, other, tail)
        ]
    theirs = lax.ppermute(other, "dp", sibling)
    token_grad, logit_grad = call(
        lambda *refs: final_kernel(held, *refs),
        [
            shape((tok_count, width), bf16),
            shape((experts, tok_count), f32),
        ],
        [VMEM] * 8,
        [],
        2 * tok_count * rows_dev * width,
        2 * width * (tok_count + rows_dev),
    )(pick, mine, theirs, tail, chosen, inv_w, inv_total, mark)
    return (token_grad, logit_grad.T, down_grad)


def solution(mesh):
    in_specs = (
        P(("expert", "dp"), None),
        P(("expert", "dp"), None),
        P(("expert", "dp"), None),
        P(("expert", "dp"), None),
        P("expert", None, None),
        P("expert", None, None),
        P("expert", None, None),
    )
    out_specs = (P(("expert", "dp"), None), P(("expert", "dp"), None), P("expert", None, "dp"))
    return jax.shard_map(
        per_device, mesh=mesh, in_specs=in_specs, out_specs=out_specs, check_vma=False
    )
```

```python
import jax
import jax.numpy as jnp
from jax import lax
from jax.experimental import pallas as pl
from jax.experimental.pallas import tpu as pltpu
from jax.sharding import PartitionSpec as P

SPLIT = 16
SCALE = 2.5
QUAD = 4
bf16 = jnp.bfloat16
f32 = jnp.float32
CONTRACT0 = (((0,), (0,)), ((), ()))
CONTRACT1 = (((1,), (1,)), ((), ()))
VMEM = pl.BlockSpec(memory_space=pltpu.VMEM)


def chunk_of(size, limit):
    best = 128
    for step in range(128, limit + 1, 128):
        if size % step == 0:
            best = step
    return best


def inner_chip():
    member = lax.rem(lax.axis_index("expert"), SPLIT) // QUAD
    return (member > 0) & (member < SPLIT // QUAD - 1)


def slot_rows(blocks):
    own, far, ends, outer, middle = [b[...] for b in blocks]
    return jnp.concatenate([own, far, ends, jnp.where(inner_chip(), middle, outer)], axis=0)


def split_of(total):
    return total // 2 // 256 * 256


def pack_kernel(gate, up, down, weights, packed, sems):
    ff = gate.shape[2]
    wide = 2 * ff
    part = packed.shape[0] * 2 // 3
    start = pl.multiple_of(lax.axis_index("dp") * part, 128)
    half = pl.ds(start, part)
    pairs = [
        (gate.at[0, half, :], packed.at[:part, :ff]),
        (up.at[0, half, :], packed.at[:part, ff:]),
    ]
    for c in range(part // wide):
        columns = pl.ds(pl.multiple_of(start + c * wide, 128), wide)
        pairs.append((down.at[0, :, columns], packed.at[part + c * ff : part + (c + 1) * ff, :]))
    reads = len(pairs)
    pairs.append((packed, weights))
    copies = [
        pltpu.make_async_copy(src, dst, sems.at[i]) for i, (src, dst) in enumerate(pairs)
    ]
    for copy in copies[:reads]:
        copy.start()
    for copy in copies[:reads]:
        copy.wait()
    for copy in copies[reads:]:
        copy.start()
    for copy in copies[reads:]:
        copy.wait()


def arrived_kernel(w1, w2, mark):
    mark[...] = jnp.zeros_like(mark)


def prep_kernel(held, capacity, *refs):
    tokens, cotangent, logits, ids = refs[:4]
    mine, other, pick_out, chosen_out, inv_w_out, inv_total_out = refs[4:]
    part = mine.shape[2]
    core = lax.axis_index("dp")
    start = pl.multiple_of(core * part, 128)
    away = pl.multiple_of((1 - core) * part, 128)

    experts, count = logits.shape
    expert = lax.broadcasted_iota(jnp.int32, (experts, count), 0)
    has = expert == ids[0:1, :]
    for k in range(1, ids.shape[0]):
        has = has | (expert == ids[k : k + 1, :])
    chosen = jnp.where(has, jax.nn.sigmoid(logits[...]), 0.0)
    total = jnp.sum(chosen, axis=0, keepdims=True)
    weight = (SCALE * chosen / total).astype(bf16).astype(f32)
    before = lax.broadcasted_iota(jnp.int32, (count, count), 0)
    after = lax.broadcasted_iota(jnp.int32, (count, count), 1)
    earlier = jnp.where(before < after, 1.0, 0.0).astype(bf16)
    named = jnp.where(has, 1.0, 0.0)
    rank = jnp.dot(named.astype(bf16), earlier, preferred_element_type=f32)
    slots = held * capacity
    slot = lax.broadcasted_iota(jnp.int32, (slots, count), 0)
    pick = jnp.zeros((slots, count), f32)
    value = jnp.zeros((slots, count), f32)
    for e in range(held):
        place = rank[e : e + 1, :].astype(jnp.int32) + e * capacity
        hit = jnp.where(slot == place, named[e : e + 1, :], 0.0)
        pick = pick + hit
        value = value + hit * weight[e : e + 1, :]
    value = jnp.sum(value, axis=1, keepdims=True)
    pick = pick.astype(bf16)
    pick_out[...] = pick
    chosen_out[...] = chosen
    inv_w_out[...] = jnp.where(has & (expert < held), 1.0 / weight, 0.0)
    inv_total_out[...] = jnp.broadcast_to(1.0 / total, chosen.shape)

    step = chunk_of(part, 512)

    def body(k, carry):
        at = pl.multiple_of(k * step, 128)
        for base, out in ((start, mine), (away, other)):
            columns = pl.ds(pl.multiple_of(base + at, 128), step)
            x = jnp.dot(pick, tokens[:, columns], preferred_element_type=f32)
            c = jnp.dot(pick, cotangent[:, columns], preferred_element_type=f32)
            out[0, :, pl.ds(at, step)] = x.astype(bf16)
            out[1, :, pl.ds(at, step)] = (c * value).astype(bf16)
        return carry

    lax.fori_loop(0, part // step, body, 0)


def sum_kernel(own, far, ends, outer, middle, mine, other, tail):
    first = lax.axis_index("dp") == 0
    inner = inner_chip()
    rows, part = mine.shape
    step = chunk_of(part, 512)

    def total(columns):
        near = jnp.where(inner, 0.0, ends[:, columns].astype(f32))
        value = own[:, columns].astype(f32) + far[:, columns].astype(f32) + near
        value = value + outer[:, columns].astype(f32) + middle[:, columns].astype(f32)
        top, low = value[:rows], value[rows:]
        return jnp.where(first, top, low), jnp.where(first, low, top)

    def body(k, carry):
        columns = pl.ds(pl.multiple_of(k * step, 128), step)
        here, there = total(columns)
        mine[:, columns] = here.astype(bf16)
        other[:, columns] = there.astype(bf16)
        return carry

    lax.fori_loop(0, part // step, body, 0)
    tail[...] = total(slice(part, part + 128))[0]


def step_of(part, split):
    for step in (512, 256):
        if part % step == 0 and split % step == 0:
            return step
    return 128


def row_specs(count, step, half):
    spec = pl.BlockSpec((count, step), lambda i: (half, i))
    return [spec] * 5


def piece_specs(step, split, wide):
    upper = split // step
    whole = pl.BlockSpec((step, wide), lambda i: (i, 0))
    top = pl.BlockSpec((step, wide), lambda i: (jnp.minimum(i, upper - 1), 0))
    low = pl.BlockSpec((step, wide), lambda i: (jnp.maximum(i - upper, 0), 0))
    return [whole, whole, whole, top, low]


def piece_blocks(pieces, upper):
    here = pl.program_id(0) < upper
    *whole, top, low = [p[...] for p in pieces]
    return whole + [jnp.where(here, top, low)]


def fetch_rows(blocks, first, rows, either, sems):
    own, far, ends, outer, middle = blocks
    count = either.shape[1]
    take = slice(first, first + count)
    targets = [rows.at[i * count : (i + 1) * count, :] for i in range(3)]
    targets += [either.at[0], either.at[1]]
    return [
        pltpu.make_async_copy(src.at[take, :], dst, sems.at[i])
        for i, (src, dst) in enumerate(zip((own, far, ends, outer, middle), targets))
    ]


def finish_rows(copies, rows, either):
    for copy in copies:
        copy.wait()
    count = either.shape[1]
    rows[3 * count :, :] = jnp.where(inner_chip(), either[1], either[0])


def gate_up_kernel(*refs):
    blocks, pieces, (out, rows) = refs[:5], refs[5:10], refs[10:]
    own, far, ends, outer, middle = blocks
    *whole, top, low = pieces
    wide = top.shape[1]
    split = top.shape[0]
    part = rows.shape[1]
    count = rows.shape[0] // (SPLIT // QUAD)
    for i, block in enumerate((own, far, ends)):
        rows[i * count : (i + 1) * count, :] = block[:count, :]
    rows[3 * count :, :] = jnp.where(inner_chip(), middle[:count, :], outer[:count, :])
    for q, w in enumerate(whole):
        out[:, q * wide : (q + 1) * wide] = jnp.dot(
            rows[...], w[:part, :], preferred_element_type=f32
        )
    out[:, 3 * wide :] = jnp.dot(
        rows[:, :split], top[...], preferred_element_type=f32
    ) + jnp.dot(rows[:, split:], low[: part - split, :], preferred_element_type=f32)


def proj_kernel(*refs):
    blocks, pieces, (out, rows, either, buffer, sems) = refs[:5], refs[5:9], refs[9:]
    height, wide = buffer.shape[1:]
    ff = wide // 2
    count = either.shape[1]
    loads = fetch_rows(blocks, count, rows, either, sems)
    copies = [
        pltpu.make_async_copy(p.at[p.shape[0] - height :, :], buffer.at[q], sems.at[5 + q])
        for q, p in enumerate(pieces)
    ]
    for copy in loads + copies:
        copy.start()
    finish_rows(loads, rows, either)
    for q in range(0, QUAD, 2):
        for copy in copies[q : q + 2]:
            copy.wait()
        w = jnp.concatenate(
            [
                jnp.concatenate(
                    [buffer[i, at : at + ff, :] for at in range(0, height, ff)], axis=1
                )
                for i in (q, q + 1)
            ],
            axis=0,
        )
        out[:, q * ff : (q + 2) * ff] = lax.dot_general(
            rows[...], w, CONTRACT1, preferred_element_type=f32
        )


def activations(mine, theirs, q, ff):
    base = 2 * q * ff
    g = mine[:, base : base + ff] + theirs[:, base : base + ff]
    u = mine[:, base + ff : base + 2 * ff] + theirs[:, base + ff : base + 2 * ff]
    sig = jax.nn.sigmoid(g)
    return g, u, sig, g * sig


def down_kernel(mine, theirs, *refs):
    blocks, outs, scratch = refs[:5], refs[5:-1], refs[-1]
    own, sent1, sent2, kept1, kept2 = outs
    ff = own.shape[0]
    half = ff // 2
    step = blocks[0].shape[1]

    @pl.when(pl.program_id(0) == 0)
    def _():
        for q in range(QUAD):
            g, u, sig, active = activations(mine, theirs, q, ff)
            hidden = (active * u).astype(bf16).astype(f32)
            scratch[q * ff : (q + 1) * ff, :] = hidden.T.astype(bf16)

    columns = pl.ds(pl.multiple_of(pl.program_id(0) * step, 128), step)
    rows = slot_rows(blocks)
    grads = jnp.dot(scratch[...], rows, preferred_element_type=f32).astype(bf16)
    g0, g1, g2, g3 = [grads[q * ff : (q + 1) * ff] for q in range(QUAD)]
    own[:, columns] = g0
    sent1[:, columns] = jnp.concatenate([g3[:half], g1[:half]], axis=0)
    sent2[:, columns] = jnp.concatenate([g3[half:], g2[half:]], axis=0)
    kept1[:, columns] = g1[half:]
    kept2[:, columns] = g2[:half]


def back_kernel(upper, mine, theirs, proj_mine, proj_theirs, *refs):
    members = SPLIT // QUAD
    pieces, outs, scratch = refs[: -members - 1], refs[-members - 1 : -1], refs[-1]
    step, wide = pieces[0].shape
    ff = wide // 2
    rows = outs[0].shape[0]
    part = outs[0].shape[1] - 128

    @pl.when(pl.program_id(0) == 0)
    def _():
        dots = 0.0
        for q in range(QUAD):
            g, u, sig, active = activations(mine, theirs, q, ff)
            proj = proj_mine[:, q * ff : (q + 1) * ff] + proj_theirs[:, q * ff : (q + 1) * ff]
            hidden = (active * u).astype(bf16).astype(f32)
            dots = dots + jnp.sum(hidden * proj, axis=1, keepdims=True)
            base = 2 * q * ff
            dgate = proj * u * sig * (1.0 + g * (1.0 - sig))
            scratch[:, base : base + ff] = dgate.astype(bf16)
            scratch[:, base + ff : base + 2 * ff] = (proj * active).astype(bf16)

        high = dots.astype(bf16).astype(f32)
        rest = dots - high
        lane = lax.broadcasted_iota(jnp.int32, (rows, 128), 1)
        for i, out in enumerate(outs):
            at = 2 if i == 2 else 0
            top, low = high[i * rows : (i + 1) * rows], rest[i * rows : (i + 1) * rows]
            out[:, part : part + 128] = jnp.where(
                lane == at, top, jnp.where(lane == at + 1, low, 0.0)
            ).astype(bf16)

    columns = pl.ds(pl.multiple_of(pl.program_id(0) * step, 128), step)
    w = jnp.concatenate(piece_blocks(pieces, upper), axis=1)
    grads = lax.dot_general(scratch[...], w, CONTRACT1, preferred_element_type=f32)
    for i, out in enumerate(outs):
        out[:, columns] = grads[i * rows : (i + 1) * rows].astype(bf16)


def final_kernel(held, pick, mine, theirs, tail, chosen, inv_w, inv_total, mark, tok_out, logit_out):
    core = lax.axis_index("dp")
    slots, part = mine.shape
    step = chunk_of(part, 512)
    pick_t = pick[...]

    def body(k, carry):
        at = pl.multiple_of(k * step, 128)
        for source, side in ((mine, core), (theirs, 1 - core)):
            block = lax.dot_general(
                pick_t, source[:, pl.ds(at, step)], CONTRACT0, preferred_element_type=f32
            )
            tok_out[:, pl.ds(pl.multiple_of(side * part + at, 128), step)] = block.astype(bf16)
        return carry

    lax.fori_loop(0, part // step, body, 0)
    values = jnp.sum(tail[...], axis=1, keepdims=True)
    entries = pick_t.astype(f32) * values
    full = chosen.shape
    expert = lax.broadcasted_iota(jnp.int32, full, 0)
    slot = lax.broadcasted_iota(jnp.int32, entries.shape, 0)
    capacity = slots // held
    dw = jnp.zeros(full, f32)
    for e in range(held):
        inside = (slot >= e * capacity) & (slot < (e + 1) * capacity)
        found = jnp.sum(jnp.where(inside, entries, 0.0), axis=0, keepdims=True)
        dw = jnp.where(expert == e, jnp.broadcast_to(found, full), dw)
    dw = dw * inv_w[...]
    share = chosen[...]
    inner = jnp.sum(dw * share, axis=0, keepdims=True) * inv_total[...]
    logit_out[...] = SCALE * inv_total[...] * (dw - inner) * share * (1.0 - share)


def call(kernel, outs, in_specs, scratch, flops, moved, limit=20, out_specs=None, grid=()):
    return pl.pallas_call(
        kernel,
        out_shape=outs,
        grid=grid,
        in_specs=in_specs,
        out_specs=out_specs or [VMEM] * len(outs),
        scratch_shapes=scratch,
        compiler_params=pltpu.CompilerParams(vmem_limit_bytes=limit * 1024 * 1024),
        cost_estimate=pl.CostEstimate(flops=flops, bytes_accessed=moved, transcendentals=0),
    )


def per_device(tokens, cotangent, logits, expert_ids, gate_proj, up_proj, down_proj):
    devices = lax.axis_size("expert")
    cores = lax.axis_size("dp")
    core = lax.axis_index("dp")
    held = devices // SPLIT
    tok_count, top = expert_ids.shape
    experts = logits.shape[1]
    width = tokens.shape[1]
    ff = gate_proj.shape[2]
    part = width // cores
    capacity = max(2, 5 * tok_count * top // (4 * experts))
    members = SPLIT // QUAD
    rows_dev = held * capacity
    rows_chip = cores * rows_dev
    slots = members * rows_chip
    across = [[e * SPLIT + j for e in range(held)] for j in range(SPLIT)]
    swap1 = [(i, i ^ 1) for i in range(devices)]
    swap2 = [(i, i ^ 2) for i in range(devices)]
    sibling = [(c, cores - 1 - c) for c in range(cores)]
    barrier = lax.optimization_barrier

    def send(array, route):
        return lax.ppermute(array, "expert", route)

    def line(pairs):
        return [
            (e * SPLIT + a * QUAD + q, e * SPLIT + b * QUAD + q)
            for e in range(held)
            for a, b in pairs
            for q in range(QUAD)
        ]

    distant = line([(m, m ^ 2) for m in range(members)])
    outward = line([(1, 0), (2, 3)])
    inward = line([(0, 1), (3, 2)])
    middle_swap = line([(1, 2), (2, 1)])
    inner = inner_chip()

    lowf = ff // 2
    packed = part + part // 2
    split = split_of(packed)
    shape = jax.ShapeDtypeStruct
    hbm = pl.BlockSpec(memory_space=pltpu.HBM)
    (weights,) = call(
        pack_kernel,
        [shape((packed, 2 * ff), bf16)],
        [hbm] * 3,
        [pltpu.VMEM((packed, 2 * ff), bf16), pltpu.SemaphoreType.DMA((3 + part // (2 * ff),))],
        0,
        12 * part * ff,
        limit=58,
        out_specs=[hbm],
    )(gate_proj, up_proj, down_proj)
    weights, logits, tokens = barrier((weights, logits, tokens))
    mine, other, pick, chosen, inv_w, inv_total = call(
        lambda *refs: prep_kernel(held, capacity, *refs),
        [shape((2, rows_dev, part), bf16)] * 2
        + [shape((rows_dev, tok_count), bf16)]
        + [shape((experts, tok_count), f32)] * 3,
        [VMEM] * 4,
        [],
        4 * rows_dev * tok_count * width,
        4 * tok_count * width,
        limit=16,
    )(tokens, cotangent, logits.T, expert_ids.T)
    w1 = send(weights, swap1)
    w2 = send(weights, swap2)

    theirs = lax.ppermute(other, "dp", sibling)
    own = jnp.concatenate(
        [
            jnp.where(core == (0 if side == 0 else cores - 1), mine[i], theirs[i])
            for i in range(2)
            for side in range(cores)
        ],
        axis=0,
    )
    if held > 1:
        own = own.reshape(2, cores, held, capacity, part)
        own = lax.all_to_all(own, "expert", 2, 2, axis_index_groups=across, tiled=True)
        own = own.reshape(2 * rows_chip, part)
    far = send(own, distant)
    outer = send(own, outward)
    (mark,) = call(
        arrived_kernel,
        [shape((8, 128), f32)],
        [pl.BlockSpec(memory_space=pl.ANY)] * 2,
        [],
        64 * slots * part * QUAD * ff,
        0,
    )(w1, w2)
    w1, w2, own, far, outer, mark = barrier((w1, w2, own, far, outer, mark))
    w3_top = send(w2[:split], swap1)
    w3_low = send(w1[split:], swap2)
    ends = send(jnp.where(inner, far, own), outward + inward)
    middle = send(own, middle_swap)
    w = [weights, w1, w2, w3_top, w3_low]
    blocks = [own, far, ends, outer, middle]

    matmul = 2 * slots * part * QUAD * ff
    step = step_of(part, split)
    upper = split // step
    grid = (part // step,)
    w_specs = piece_specs(step, split, 2 * ff)
    anywhere = pl.BlockSpec(memory_space=pl.ANY)
    row_scratch = [
        pltpu.VMEM((slots, part), bf16),
        pltpu.VMEM((2, rows_chip, part), bf16),
    ]
    (g_u,) = call(
        gate_up_kernel,
        [shape((slots, QUAD * 2 * ff), f32)],
        [VMEM] * 10,
        row_scratch[:1],
        2 * matmul,
        2 * part * (slots + QUAD * 2 * ff),
    )(*blocks, *w)
    g_u_sib = lax.ppermute(g_u, "dp", sibling)
    (proj,) = call(
        proj_kernel,
        [shape((slots, QUAD * ff), f32)],
        [anywhere] * 9,
        row_scratch + [pltpu.VMEM((QUAD, part // 2, 2 * ff), bf16), pltpu.SemaphoreType.DMA((9,))],
        matmul,
        2 * part * (slots + QUAD * ff),
    )(*blocks, weights, w1, w2, w3_low)
    proj_sib = lax.ppermute(proj, "dp", sibling)
    g0, sent1, sent2, kept1, kept2 = call(
        down_kernel,
        [shape((ff, part), bf16)] * 3 + [shape((lowf, part), bf16)] * 2,
        [VMEM] * 2 + row_specs(rows_chip, step, 1),
        [pltpu.VMEM((QUAD * ff, slots), bf16)],
        matmul,
        2 * part * (slots + QUAD * ff),
        grid=grid,
    )(g_u, g_u_sib, *blocks)
    g0, sent1, sent2, proj, proj_sib = barrier((g0, sent1, sent2, proj, proj_sib))
    got1 = send(sent1, swap1)
    got2 = send(sent2, swap2)
    b0, b1, b2, b3 = call(
        lambda *refs: back_kernel(upper, *refs),
        [shape((rows_chip, part + 128), bf16)] * members,
        [VMEM] * 4 + w_specs,
        [pltpu.VMEM((slots, QUAD * 2 * ff), bf16)],
        2 * matmul,
        2 * part * (slots + QUAD * 2 * ff),
        grid=grid,
    )(g_u, g_u_sib, proj, proj_sib, *w)

    ends = send(b2, outward + inward)
    middle = send(b3, middle_swap)
    ends, middle, got1, got2, b1, b3 = barrier((ends, middle, got1, got2, b1, b3))
    joined = b1 + jnp.where(inner, ends, jnp.zeros((), bf16))
    joined, got1, got2 = barrier((joined, got1, got2))
    far = send(joined, distant)
    outer = send(b3, inward)
    got3 = send(kept1 + got2[:lowf], swap1)
    got4 = send(kept2 + got1[:lowf], swap2)
    mine, other, tail = call(
        sum_kernel,
        [shape((rows_dev, part), bf16)] * 2 + [shape((rows_dev, 128), f32)],
        [VMEM] * 5,
        [],
        matmul,
        12 * rows_chip * part,
    )(b0, far, ends, outer, middle)
    other, got3, got4 = barrier((other, got3, got4))
    add = lambda a, b, c: (a.astype(f32) + b.astype(f32) + c.astype(f32)).astype(bf16)
    down_grad = jnp.concatenate(
        [add(g0[:lowf], got1[lowf:], got4), add(g0[lowf:], got2[lowf:], got3)], axis=0
    )[None]
    if held > 1:
        mine, other, tail = [
            lax.all_to_all(
                array.reshape(held, capacity, array.shape[1]),
                "expert",
                0,
                0,
                axis_index_groups=across,
                tiled=True,
            ).reshape(array.shape)
            for array in (mine, other, tail)
        ]
    theirs = lax.ppermute(other, "dp", sibling)
    token_grad, logit_grad = call(
        lambda *refs: final_kernel(held, *refs),
        [
            shape((tok_count, width), bf16),
            shape((experts, tok_count), f32),
        ],
        [VMEM] * 8,
        [],
        2 * tok_count * rows_dev * width,
        2 * width * (tok_count + rows_dev),
    )(pick, mine, theirs, tail, chosen, inv_w, inv_total, mark)
    return (token_grad, logit_grad.T, down_grad)


def solution(mesh):
    in_specs = (
        P(("expert", "dp"), None),
        P(("expert", "dp"), None),
        P(("expert", "dp"), None),
        P(("expert", "dp"), None),
        P("expert", None, None),
        P("expert", None, None),
        P("expert", None, None),
    )
    out_specs = (P(("expert", "dp"), None), P(("expert", "dp"), None), P("expert", None, "dp"))
    return jax.shard_map(
        per_device, mesh=mesh, in_specs=in_specs, out_specs=out_specs, check_vma=False
    )
```

```python
import jax
import jax.numpy as jnp
from jax import lax
from jax.experimental import pallas as pl
from jax.experimental.pallas import tpu as pltpu
from jax.sharding import PartitionSpec as P

SPLIT = 16
SCALE = 2.5
QUAD = 4
bf16 = jnp.bfloat16
f32 = jnp.float32
CONTRACT0 = (((0,), (0,)), ((), ()))
CONTRACT1 = (((1,), (1,)), ((), ()))
VMEM = pl.BlockSpec(memory_space=pltpu.VMEM)


def chunk_of(size, limit):
    best = 128
    for step in range(128, limit + 1, 128):
        if size % step == 0:
            best = step
    return best


def inner_chip():
    member = lax.rem(lax.axis_index("expert"), SPLIT) // QUAD
    return (member > 0) & (member < SPLIT // QUAD - 1)


def slot_rows(blocks):
    own, far, ends, outer, middle = [b[...] for b in blocks]
    return jnp.concatenate([own, far, ends, jnp.where(inner_chip(), middle, outer)], axis=0)


def split_of(total):
    return total // 2 // 256 * 256


def pack_kernel(gate, up, down, weights, packed, sems):
    ff = gate.shape[2]
    wide = 2 * ff
    part = packed.shape[0] * 2 // 3
    start = pl.multiple_of(lax.axis_index("dp") * part, 128)
    half = pl.ds(start, part)
    pairs = [
        (gate.at[0, half, :], packed.at[:part, :ff]),
        (up.at[0, half, :], packed.at[:part, ff:]),
    ]
    for c in range(part // wide):
        columns = pl.ds(pl.multiple_of(start + c * wide, 128), wide)
        pairs.append((down.at[0, :, columns], packed.at[part + c * ff : part + (c + 1) * ff, :]))
    reads = len(pairs)
    pairs.append((packed, weights))
    copies = [
        pltpu.make_async_copy(src, dst, sems.at[i]) for i, (src, dst) in enumerate(pairs)
    ]
    for copy in copies[:reads]:
        copy.start()
    for copy in copies[:reads]:
        copy.wait()
    for copy in copies[reads:]:
        copy.start()
    for copy in copies[reads:]:
        copy.wait()


def arrived_kernel(w1, w2, mark):
    mark[...] = jnp.zeros_like(mark)


def prep_kernel(held, capacity, *refs):
    tokens, cotangent, logits, ids = refs[:4]
    mine, other, pick_out, chosen_out, inv_w_out, inv_total_out = refs[4:]
    part = mine.shape[2]
    core = lax.axis_index("dp")
    start = pl.multiple_of(core * part, 128)
    away = pl.multiple_of((1 - core) * part, 128)

    experts, count = logits.shape
    expert = lax.broadcasted_iota(jnp.int32, (experts, count), 0)
    has = expert == ids[0:1, :]
    for k in range(1, ids.shape[0]):
        has = has | (expert == ids[k : k + 1, :])
    chosen = jnp.where(has, jax.nn.sigmoid(logits[...]), 0.0)
    total = jnp.sum(chosen, axis=0, keepdims=True)
    weight = (SCALE * chosen / total).astype(bf16).astype(f32)
    before = lax.broadcasted_iota(jnp.int32, (count, count), 0)
    after = lax.broadcasted_iota(jnp.int32, (count, count), 1)
    earlier = jnp.where(before < after, 1.0, 0.0).astype(bf16)
    named = jnp.where(has, 1.0, 0.0)
    rank = jnp.dot(named.astype(bf16), earlier, preferred_element_type=f32)
    slots = held * capacity
    slot = lax.broadcasted_iota(jnp.int32, (slots, count), 0)
    pick = jnp.zeros((slots, count), f32)
    value = jnp.zeros((slots, count), f32)
    for e in range(held):
        place = rank[e : e + 1, :].astype(jnp.int32) + e * capacity
        hit = jnp.where(slot == place, named[e : e + 1, :], 0.0)
        pick = pick + hit
        value = value + hit * weight[e : e + 1, :]
    value = jnp.sum(value, axis=1, keepdims=True)
    pick = pick.astype(bf16)
    pick_out[...] = pick
    chosen_out[...] = chosen
    inv_w_out[...] = jnp.where(has & (expert < held), 1.0 / weight, 0.0)
    inv_total_out[...] = jnp.broadcast_to(1.0 / total, chosen.shape)

    step = chunk_of(part, 512)

    def body(k, carry):
        at = pl.multiple_of(k * step, 128)
        for base, out in ((start, mine), (away, other)):
            columns = pl.ds(pl.multiple_of(base + at, 128), step)
            x = jnp.dot(pick, tokens[:, columns], preferred_element_type=f32)
            c = jnp.dot(pick, cotangent[:, columns], preferred_element_type=f32)
            out[0, :, pl.ds(at, step)] = x.astype(bf16)
            out[1, :, pl.ds(at, step)] = (c * value).astype(bf16)
        return carry

    lax.fori_loop(0, part // step, body, 0)


def sum_kernel(own, far, ends, outer, middle, mine, other, tail):
    first = lax.axis_index("dp") == 0
    inner = inner_chip()
    rows, part = mine.shape
    step = chunk_of(part, 512)

    def total(columns):
        near = jnp.where(inner, 0.0, ends[:, columns].astype(f32))
        value = own[:, columns].astype(f32) + far[:, columns].astype(f32) + near
        value = value + outer[:, columns].astype(f32) + middle[:, columns].astype(f32)
        top, low = value[:rows], value[rows:]
        return jnp.where(first, top, low), jnp.where(first, low, top)

    def body(k, carry):
        columns = pl.ds(pl.multiple_of(k * step, 128), step)
        here, there = total(columns)
        mine[:, columns] = here.astype(bf16)
        other[:, columns] = there.astype(bf16)
        return carry

    lax.fori_loop(0, part // step, body, 0)
    tail[...] = total(slice(part, part + 128))[0]


def step_of(part, split):
    for step in (512, 256):
        if part % step == 0 and split % step == 0:
            return step
    return 128


def row_specs(count, step, half):
    spec = pl.BlockSpec((count, step), lambda i: (half, i))
    return [spec] * 5


def piece_specs(step, split, wide):
    upper = split // step
    whole = pl.BlockSpec((step, wide), lambda i: (i, 0))
    top = pl.BlockSpec((step, wide), lambda i: (jnp.minimum(i, upper - 1), 0))
    low = pl.BlockSpec((step, wide), lambda i: (jnp.maximum(i - upper, 0), 0))
    return [whole, whole, whole, top, low]


def piece_blocks(pieces, upper, step):
    i = pl.program_id(0)
    at = [i, i, i, jnp.minimum(i, upper - 1), jnp.maximum(i - upper, 0)]
    here = pl.program_id(0) < upper
    *whole, top, low = [
        p[pl.ds(pl.multiple_of(k * step, 128), step), :] for p, k in zip(pieces, at)
    ]
    return whole + [jnp.where(here, top, low)]


def fetch_rows(blocks, first, rows, either, sems):
    own, far, ends, outer, middle = blocks
    count = either.shape[1]
    take = slice(first, first + count)
    targets = [rows.at[i * count : (i + 1) * count, :] for i in range(3)]
    targets += [either.at[0], either.at[1]]
    return [
        pltpu.make_async_copy(src.at[take, :], dst, sems.at[i])
        for i, (src, dst) in enumerate(zip((own, far, ends, outer, middle), targets))
    ]


def finish_rows(copies, rows, either):
    for copy in copies:
        copy.wait()
    count = either.shape[1]
    rows[3 * count :, :] = jnp.where(inner_chip(), either[1], either[0])


def gate_up_kernel(*refs):
    blocks, pieces, (out, rows) = refs[:5], refs[5:10], refs[10:]
    own, far, ends, outer, middle = blocks
    *whole, top, low = pieces
    wide = top.shape[1]
    split = top.shape[0]
    part = rows.shape[1]
    count = rows.shape[0] // (SPLIT // QUAD)
    for i, block in enumerate((own, far, ends)):
        rows[i * count : (i + 1) * count, :] = block[:count, :]
    rows[3 * count :, :] = jnp.where(inner_chip(), middle[:count, :], outer[:count, :])
    for q, w in enumerate(whole):
        out[:, q * wide : (q + 1) * wide] = jnp.dot(
            rows[...], w[:part, :], preferred_element_type=f32
        )
    out[:, 3 * wide :] = jnp.dot(
        rows[:, :split], top[...], preferred_element_type=f32
    ) + jnp.dot(rows[:, split:], low[: part - split, :], preferred_element_type=f32)


def proj_kernel(*refs):
    blocks, pieces, (out, rows, either, buffer, sems) = refs[:5], refs[5:9], refs[9:]
    height, wide = buffer.shape[1:]
    ff = wide // 2
    count = either.shape[1]
    loads = fetch_rows(blocks, count, rows, either, sems)
    copies = [
        pltpu.make_async_copy(p.at[p.shape[0] - height :, :], buffer.at[q], sems.at[5 + q])
        for q, p in enumerate(pieces)
    ]
    for copy in loads + copies:
        copy.start()
    finish_rows(loads, rows, either)
    for q in range(0, QUAD, 2):
        for copy in copies[q : q + 2]:
            copy.wait()
        w = jnp.concatenate(
            [
                jnp.concatenate(
                    [buffer[i, at : at + ff, :] for at in range(0, height, ff)], axis=1
                )
                for i in (q, q + 1)
            ],
            axis=0,
        )
        out[:, q * ff : (q + 2) * ff] = lax.dot_general(
            rows[...], w, CONTRACT1, preferred_element_type=f32
        )


def activations(mine, theirs, q, ff):
    base = 2 * q * ff
    g = mine[:, base : base + ff] + theirs[:, base : base + ff]
    u = mine[:, base + ff : base + 2 * ff] + theirs[:, base + ff : base + 2 * ff]
    sig = jax.nn.sigmoid(g)
    return g, u, sig, g * sig


def down_kernel(mine, theirs, *refs):
    blocks, outs, scratch = refs[:5], refs[5:-1], refs[-1]
    own, sent1, sent2, kept1, kept2 = outs
    ff = own.shape[0]
    half = ff // 2
    step = blocks[0].shape[1]

    @pl.when(pl.program_id(0) == 0)
    def _():
        for q in range(QUAD):
            g, u, sig, active = activations(mine, theirs, q, ff)
            hidden = (active * u).astype(bf16).astype(f32)
            scratch[q * ff : (q + 1) * ff, :] = hidden.T.astype(bf16)

    columns = pl.ds(pl.multiple_of(pl.program_id(0) * step, 128), step)
    rows = slot_rows(blocks)
    grads = jnp.dot(scratch[...], rows, preferred_element_type=f32).astype(bf16)
    g0, g1, g2, g3 = [grads[q * ff : (q + 1) * ff] for q in range(QUAD)]
    own[:, columns] = g0
    sent1[:, columns] = jnp.concatenate([g3[:half], g1[:half]], axis=0)
    sent2[:, columns] = jnp.concatenate([g3[half:], g2[half:]], axis=0)
    kept1[:, columns] = g1[half:]
    kept2[:, columns] = g2[:half]


def back_kernel(upper, step, mine, theirs, proj_mine, proj_theirs, *refs):
    members = SPLIT // QUAD
    pieces, outs, scratch = refs[: -members - 1], refs[-members - 1 : -1], refs[-1]
    wide = pieces[0].shape[1]
    ff = wide // 2
    rows = outs[0].shape[0]
    part = outs[0].shape[1] - 128

    @pl.when(pl.program_id(0) == 0)
    def _():
        dots = 0.0
        for q in range(QUAD):
            g, u, sig, active = activations(mine, theirs, q, ff)
            proj = proj_mine[:, q * ff : (q + 1) * ff] + proj_theirs[:, q * ff : (q + 1) * ff]
            hidden = (active * u).astype(bf16).astype(f32)
            dots = dots + jnp.sum(hidden * proj, axis=1, keepdims=True)
            base = 2 * q * ff
            dgate = proj * u * sig * (1.0 + g * (1.0 - sig))
            scratch[:, base : base + ff] = dgate.astype(bf16)
            scratch[:, base + ff : base + 2 * ff] = (proj * active).astype(bf16)

        high = dots.astype(bf16).astype(f32)
        rest = dots - high
        lane = lax.broadcasted_iota(jnp.int32, (rows, 128), 1)
        for i, out in enumerate(outs):
            at = 2 if i == 2 else 0
            top, low = high[i * rows : (i + 1) * rows], rest[i * rows : (i + 1) * rows]
            out[:, part : part + 128] = jnp.where(
                lane == at, top, jnp.where(lane == at + 1, low, 0.0)
            ).astype(bf16)

    columns = pl.ds(pl.multiple_of(pl.program_id(0) * step, 128), step)
    w = jnp.concatenate(piece_blocks(pieces, upper, step), axis=1)
    grads = lax.dot_general(scratch[...], w, CONTRACT1, preferred_element_type=f32)
    for i, out in enumerate(outs):
        out[:, columns] = grads[i * rows : (i + 1) * rows].astype(bf16)


def final_kernel(held, pick, mine, theirs, tail, chosen, inv_w, inv_total, mark, tok_out, logit_out):
    core = lax.axis_index("dp")
    slots, part = mine.shape
    step = chunk_of(part, 512)
    pick_t = pick[...]

    def body(k, carry):
        at = pl.multiple_of(k * step, 128)
        for source, side in ((mine, core), (theirs, 1 - core)):
            block = lax.dot_general(
                pick_t, source[:, pl.ds(at, step)], CONTRACT0, preferred_element_type=f32
            )
            tok_out[:, pl.ds(pl.multiple_of(side * part + at, 128), step)] = block.astype(bf16)
        return carry

    lax.fori_loop(0, part // step, body, 0)
    values = jnp.sum(tail[...], axis=1, keepdims=True)
    entries = pick_t.astype(f32) * values
    full = chosen.shape
    expert = lax.broadcasted_iota(jnp.int32, full, 0)
    slot = lax.broadcasted_iota(jnp.int32, entries.shape, 0)
    capacity = slots // held
    dw = jnp.zeros(full, f32)
    for e in range(held):
        inside = (slot >= e * capacity) & (slot < (e + 1) * capacity)
        found = jnp.sum(jnp.where(inside, entries, 0.0), axis=0, keepdims=True)
        dw = jnp.where(expert == e, jnp.broadcast_to(found, full), dw)
    dw = dw * inv_w[...]
    share = chosen[...]
    inner = jnp.sum(dw * share, axis=0, keepdims=True) * inv_total[...]
    logit_out[...] = SCALE * inv_total[...] * (dw - inner) * share * (1.0 - share)


def call(kernel, outs, in_specs, scratch, flops, moved, limit=20, out_specs=None, grid=()):
    return pl.pallas_call(
        kernel,
        out_shape=outs,
        grid=grid,
        in_specs=in_specs,
        out_specs=out_specs or [VMEM] * len(outs),
        scratch_shapes=scratch,
        compiler_params=pltpu.CompilerParams(vmem_limit_bytes=limit * 1024 * 1024),
        cost_estimate=pl.CostEstimate(flops=flops, bytes_accessed=moved, transcendentals=0),
    )


def per_device(tokens, cotangent, logits, expert_ids, gate_proj, up_proj, down_proj):
    devices = lax.axis_size("expert")
    cores = lax.axis_size("dp")
    core = lax.axis_index("dp")
    held = devices // SPLIT
    tok_count, top = expert_ids.shape
    experts = logits.shape[1]
    width = tokens.shape[1]
    ff = gate_proj.shape[2]
    part = width // cores
    capacity = max(2, 5 * tok_count * top // (4 * experts))
    members = SPLIT // QUAD
    rows_dev = held * capacity
    rows_chip = cores * rows_dev
    slots = members * rows_chip
    across = [[e * SPLIT + j for e in range(held)] for j in range(SPLIT)]
    swap1 = [(i, i ^ 1) for i in range(devices)]
    swap2 = [(i, i ^ 2) for i in range(devices)]
    sibling = [(c, cores - 1 - c) for c in range(cores)]
    barrier = lax.optimization_barrier

    def send(array, route):
        return lax.ppermute(array, "expert", route)

    def line(pairs):
        return [
            (e * SPLIT + a * QUAD + q, e * SPLIT + b * QUAD + q)
            for e in range(held)
            for a, b in pairs
            for q in range(QUAD)
        ]

    distant = line([(m, m ^ 2) for m in range(members)])
    outward = line([(1, 0), (2, 3)])
    inward = line([(0, 1), (3, 2)])
    middle_swap = line([(1, 2), (2, 1)])
    inner = inner_chip()

    lowf = ff // 2
    packed = part + part // 2
    split = split_of(packed)
    shape = jax.ShapeDtypeStruct
    hbm = pl.BlockSpec(memory_space=pltpu.HBM)
    (weights,) = call(
        pack_kernel,
        [shape((packed, 2 * ff), bf16)],
        [hbm] * 3,
        [pltpu.VMEM((packed, 2 * ff), bf16), pltpu.SemaphoreType.DMA((3 + part // (2 * ff),))],
        0,
        12 * part * ff,
        limit=58,
        out_specs=[hbm],
    )(gate_proj, up_proj, down_proj)
    weights, logits, tokens = barrier((weights, logits, tokens))
    mine, other, pick, chosen, inv_w, inv_total = call(
        lambda *refs: prep_kernel(held, capacity, *refs),
        [shape((2, rows_dev, part), bf16)] * 2
        + [shape((rows_dev, tok_count), bf16)]
        + [shape((experts, tok_count), f32)] * 3,
        [VMEM] * 4,
        [],
        4 * rows_dev * tok_count * width,
        4 * tok_count * width,
        limit=16,
    )(tokens, cotangent, logits.T, expert_ids.T)
    w1 = send(weights, swap1)
    w2 = send(weights, swap2)

    theirs = lax.ppermute(other, "dp", sibling)
    own = jnp.concatenate(
        [
            jnp.where(core == (0 if side == 0 else cores - 1), mine[i], theirs[i])
            for i in range(2)
            for side in range(cores)
        ],
        axis=0,
    )
    if held > 1:
        own = own.reshape(2, cores, held, capacity, part)
        own = lax.all_to_all(own, "expert", 2, 2, axis_index_groups=across, tiled=True)
        own = own.reshape(2 * rows_chip, part)
    far = send(own, distant)
    outer = send(own, outward)
    (mark,) = call(
        arrived_kernel,
        [shape((8, 128), f32)],
        [pl.BlockSpec(memory_space=pl.ANY)] * 2,
        [],
        64 * slots * part * QUAD * ff,
        0,
    )(w1, w2)
    w1, w2, own, far, outer, mark = barrier((w1, w2, own, far, outer, mark))
    w3_top = send(w2[:split], swap1)
    w3_low = send(w1[split:], swap2)
    ends = send(jnp.where(inner, far, own), outward + inward)
    middle = send(own, middle_swap)
    w = [weights, w1, w2, w3_top, w3_low]
    blocks = [own, far, ends, outer, middle]

    matmul = 2 * slots * part * QUAD * ff
    step = step_of(part, split)
    upper = split // step
    grid = (part // step,)
    anywhere = pl.BlockSpec(memory_space=pl.ANY)
    row_scratch = [
        pltpu.VMEM((slots, part), bf16),
        pltpu.VMEM((2, rows_chip, part), bf16),
    ]
    (g_u,) = call(
        gate_up_kernel,
        [shape((slots, QUAD * 2 * ff), f32)],
        [VMEM] * 10,
        row_scratch[:1],
        2 * matmul,
        2 * part * (slots + QUAD * 2 * ff),
    )(*blocks, *w)
    g_u_sib = lax.ppermute(g_u, "dp", sibling)
    (proj,) = call(
        proj_kernel,
        [shape((slots, QUAD * ff), f32)],
        [anywhere] * 9,
        row_scratch + [pltpu.VMEM((QUAD, part // 2, 2 * ff), bf16), pltpu.SemaphoreType.DMA((9,))],
        matmul,
        2 * part * (slots + QUAD * ff),
    )(*blocks, weights, w1, w2, w3_low)
    proj_sib = lax.ppermute(proj, "dp", sibling)
    g0, sent1, sent2, kept1, kept2 = call(
        down_kernel,
        [shape((ff, part), bf16)] * 3 + [shape((lowf, part), bf16)] * 2,
        [VMEM] * 2 + row_specs(rows_chip, step, 1),
        [pltpu.VMEM((QUAD * ff, slots), bf16)],
        matmul,
        2 * part * (slots + QUAD * ff),
        grid=grid,
    )(g_u, g_u_sib, *blocks)
    g0, sent1, sent2, proj, proj_sib = barrier((g0, sent1, sent2, proj, proj_sib))
    got1 = send(sent1, swap1)
    got2 = send(sent2, swap2)
    b0, b1, b2, b3 = call(
        lambda *refs: back_kernel(upper, step, *refs),
        [shape((rows_chip, part + 128), bf16)] * members,
        [VMEM] * 9,
        [pltpu.VMEM((slots, QUAD * 2 * ff), bf16)],
        2 * matmul,
        2 * part * (slots + QUAD * 2 * ff),
        grid=grid,
    )(g_u, g_u_sib, proj, proj_sib, *w)

    ends = send(b2, outward + inward)
    middle = send(b3, middle_swap)
    ends, middle, got1, got2, b1, b3 = barrier((ends, middle, got1, got2, b1, b3))
    joined = b1 + jnp.where(inner, ends, jnp.zeros((), bf16))
    joined, got1, got2 = barrier((joined, got1, got2))
    far = send(joined, distant)
    outer = send(b3, inward)
    got3 = send(kept1 + got2[:lowf], swap1)
    got4 = send(kept2 + got1[:lowf], swap2)
    mine, other, tail = call(
        sum_kernel,
        [shape((rows_dev, part), bf16)] * 2 + [shape((rows_dev, 128), f32)],
        [VMEM] * 5,
        [],
        matmul,
        12 * rows_chip * part,
    )(b0, far, ends, outer, middle)
    other, got3, got4 = barrier((other, got3, got4))
    add = lambda a, b, c: (a.astype(f32) + b.astype(f32) + c.astype(f32)).astype(bf16)
    down_grad = jnp.concatenate(
        [add(g0[:lowf], got1[lowf:], got4), add(g0[lowf:], got2[lowf:], got3)], axis=0
    )[None]
    if held > 1:
        mine, other, tail = [
            lax.all_to_all(
                array.reshape(held, capacity, array.shape[1]),
                "expert",
                0,
                0,
                axis_index_groups=across,
                tiled=True,
            ).reshape(array.shape)
            for array in (mine, other, tail)
        ]
    theirs = lax.ppermute(other, "dp", sibling)
    token_grad, logit_grad = call(
        lambda *refs: final_kernel(held, *refs),
        [
            shape((tok_count, width), bf16),
            shape((experts, tok_count), f32),
        ],
        [VMEM] * 8,
        [],
        2 * tok_count * rows_dev * width,
        2 * width * (tok_count + rows_dev),
    )(pick, mine, theirs, tail, chosen, inv_w, inv_total, mark)
    return (token_grad, logit_grad.T, down_grad)


def solution(mesh):
    in_specs = (
        P(("expert", "dp"), None),
        P(("expert", "dp"), None),
        P(("expert", "dp"), None),
        P(("expert", "dp"), None),
        P("expert", None, None),
        P("expert", None, None),
        P("expert", None, None),
    )
    out_specs = (P(("expert", "dp"), None), P(("expert", "dp"), None), P("expert", None, "dp"))
    return jax.shard_map(
        per_device, mesh=mesh, in_specs=in_specs, out_specs=out_specs, check_vma=False
    )
```
